128 devices in a mesh: pts: 32 (over x, y, core), mdl: 4 (over z).
Axes of the slice: x: 4, y: 4, z: 4, core: 2. Of those that a mesh axis runs over, the one named last changes fastest.
Arguments:
- points: bfloat16 [65536, 256], P(('pts', 'mdl')), may hold values from -6 to 6
- to_hilbert: int32 [65536], P(('pts', 'mdl')), may hold values from 0 to 65535, as said below
- parent: int32 [65536], P(('pts', 'mdl')), may hold values from 0 to 32767, as said below
- w_qkv: bfloat16 [256, 768], replicated
- w_out: bfloat16 [256, 256], replicated, may hold values from -0.375 to 0.375
- w_pool: bfloat16 [256, 512], replicated, may hold values from -0.375 to 0.375
- w_up: bfloat16 [512, 256], replicated, may hold values from -0.25 to 0.25
- w_skip: bfloat16 [256, 256], replicated, may hold values from -0.375 to 0.375
Outputs:
- pooled: bfloat16 [32768, 512], P(('pts', 'mdl'))
- decoded: bfloat16 [65536, 256], P(('pts', 'mdl'))
The draws below stay inside these ranges and needn't reach their ends.
Inputs may be any that keep to these rules, and one draw needn't show every extreme that they name: `to_hilbert`: A permutation of the points. Of the 512 points of one device, at most 8 have Hilbert positions on any one device (positions are held 512 a device in order), and some pair of devices reaches 8. `parent`: never decreases along the points; every pooled index has at least one point. Pooled indices are held 256 a device in order; the points of a device belong to that device's pooled indices, except at most two leading points that belong to the last pooled index of the device before; some device has two such points.
All inputs are finite; a program needn't handle non-finite values.
Results may differ from the reference program's by a relative error of at most 0.02.
Values may be sent and summed in bfloat16 or wider, within the bound.
A program may use at most 64 MiB of HBM per device.

```python
import jax
import jax.numpy as jnp
from jax import lax

C = 256
C2 = 512
HEADS = 16
PATCH = 1024
ROWS_DEV = 512
POINTS = 65536
POOLED = 32768


def draw_to_hilbert(key, part):
    key = jax.random.fold_in(key, 11)
    device_total = POINTS // ROWS_DEV
    half_size = ROWS_DEV // device_total
    first_key, second_key, third_key, fourth_key = jax.random.split(key, 4)
    shifts_one = jax.random.permutation(first_key, device_total).astype(jnp.int32)
    shifts_two = jax.random.permutation(second_key, device_total).astype(jnp.int32)
    leading = shifts_one[0]
    shifts_two = jnp.where(shifts_two == leading, shifts_two[0], shifts_two)
    shifts_two = shifts_two.at[0].set(leading)
    shifts = jnp.concatenate([shifts_one[:device_total // 2], shifts_two[:device_total // 2]])
    source_order = jax.vmap(lambda item: jax.random.permutation(item, ROWS_DEV))(jax.random.split(third_key, device_total)).astype(jnp.int32)
    target_order = jax.vmap(lambda item: jax.random.permutation(item, ROWS_DEV))(jax.random.split(fourth_key, device_total)).astype(jnp.int32)
    source_dev = jnp.arange(device_total, dtype=jnp.int32)[:, None]
    position = jnp.arange(ROWS_DEV, dtype=jnp.int32)[None, :]
    target_dev = (source_dev + shifts[position // half_size]) % device_total
    source_row = source_dev * ROWS_DEV + source_order
    target_row = target_dev * ROWS_DEV + target_order[target_dev, jnp.broadcast_to(position, target_dev.shape)]
    result = jnp.zeros((POINTS,), jnp.int32).at[source_row.reshape(-1)].set(target_row.reshape(-1))
    return result


def draw_parent(key, part):
    key = jax.random.fold_in(key, 23)
    device_total = POINTS // ROWS_DEV
    cluster_count = ROWS_DEV // 2
    first_key, second_key, third_key = jax.random.split(key, 3)
    leading = jax.random.randint(first_key, (device_total,), 0, 3).astype(jnp.int32)
    leading = leading.at[0].set(0).at[1].set(2)
    trailing = jnp.concatenate([leading[1:], jnp.zeros((1,), jnp.int32)])
    first_pair = 4 + trailing - leading
    opening = 1 + jax.random.randint(second_key, (device_total,), 0, first_pair - 1).astype(jnp.int32)
    wobble = jax.random.randint(third_key, (device_total, cluster_count // 2), -1, 2).astype(jnp.int32)
    cluster_sizes = jnp.stack([2 + wobble, 2 - wobble], axis=-1).reshape(device_total, cluster_count)
    cluster_sizes = cluster_sizes.at[:, 0].set(opening).at[:, 1].set(first_pair - opening)
    cluster_sizes = cluster_sizes.at[:, cluster_count - 2].set(1).at[:, cluster_count - 1].set(3)
    starts = jnp.cumsum(cluster_sizes, axis=1) - cluster_sizes
    offsets = jnp.arange(ROWS_DEV, dtype=jnp.int32)[None, :] - leading[:, None]
    found = jax.vmap(lambda table, probe: jnp.searchsorted(table, probe, side='right'))(starts, offsets).astype(jnp.int32) - 1
    device_base = jnp.arange(device_total, dtype=jnp.int32)[:, None] * cluster_count
    result = jnp.where(offsets < 0, device_base - 1, device_base + found)
    return result.reshape(-1).astype(jnp.int32)


def draw_w_qkv(key, part):
    key = jax.random.fold_in(key, 37)
    first_key, second_key = jax.random.split(key)
    base = jax.random.normal(first_key, (C, 3 * C), jnp.float32) * C ** (-0.5)
    lower, upper = (0.8, 2.0)
    spread = jax.random.uniform(second_key, (2, HEADS), jnp.float32)
    factor = jnp.exp(jnp.log(lower) + spread * (jnp.log(upper) - jnp.log(lower)))
    head_width = C // HEADS
    column_factor = jnp.concatenate([jnp.repeat(factor[0], head_width), jnp.repeat(factor[1], head_width), jnp.ones((C,), jnp.float32)])
    return (base * column_factor[None, :]).astype(jnp.bfloat16)


def block_scale(stream_key, dims, pieces, smallest, largest):
    loudness, own = 1.0, jax.random.fold_in(stream_key, 6)
    for axis_at, parts in pieces:
        steps = jnp.exp(jax.random.uniform(jax.random.fold_in(own, axis_at), (parts,), jnp.float32, smallest / len(pieces), largest / len(pieces)))
        loudness = loudness * jnp.repeat(steps, dims[axis_at] // parts).reshape([-1 if axis == axis_at else 1 for axis in range(len(dims))])
    return loudness


def bell_draw(rng, extent, scale, reach, cuts=(), kind=jnp.bfloat16):
    values = jax.random.normal(rng, extent, jnp.float32) * scale
    if len(cuts) > 0:
        values = block_scale(rng, extent, cuts, -0.22, 0.18) * values
    return jnp.clip(values, min=-reach, max=reach).astype(kind)


def setup_inputs(seed: int = 0) -> dict:
    arg_keys = jax.random.split(jax.random.key(seed), 9)
    return {
        "points": bell_draw(arg_keys[0], (POINTS, C), 1.0, 6.0, ((0, 128),)),
        "to_hilbert": draw_to_hilbert(jax.random.fold_in(arg_keys[8], 71), 0),
        "parent": draw_parent(jax.random.fold_in(arg_keys[8], 71), 0),
        "w_qkv": draw_w_qkv(jax.random.fold_in(arg_keys[8], 71), 0),
        "w_out": bell_draw(arg_keys[4], (C, C), C ** -0.5, 0.375),
        "w_pool": bell_draw(arg_keys[5], (C, C2), C ** -0.5, 0.375),
        "w_up": bell_draw(arg_keys[6], (C2, C), C2 ** -0.5, 0.25),
        "w_skip": bell_draw(arg_keys[7], (C, C), C ** -0.5, 0.375),
    }


epsilon = 1e-05

def layer_norm(values):
    center = values - lax.optimization_barrier(jnp.mean(values, axis=-1, keepdims=True))
    spread = lax.optimization_barrier(jnp.mean(center * center, axis=-1, keepdims=True))
    return center * lax.rsqrt(spread + epsilon)

def reference(points, to_hilbert, parent, w_qkv, w_out, w_pool, w_up, w_skip):
    point_total = points.shape[0]
    head_width = C // HEADS
    score_scale = head_width ** (-0.5)
    ordered = jnp.zeros_like(points).at[to_hilbert].set(points)
    normed = layer_norm(ordered.astype(jnp.float32)).astype(jnp.bfloat16)
    projected = jnp.dot(normed, w_qkv, preferred_element_type=jnp.float32).astype(jnp.bfloat16)
    projected = projected.reshape(point_total // PATCH, PATCH, 3, HEADS, head_width)

    def attend(patch_block):
        query = patch_block[:, 0].astype(jnp.float32)
        keys = patch_block[:, 1].astype(jnp.float32)
        values = patch_block[:, 2].astype(jnp.float32)
        scores = jnp.einsum('qhd,khd->hqk', query, keys) * score_scale
        probs = jax.nn.softmax(scores, axis=-1).astype(jnp.bfloat16)
        result = jnp.einsum('hqk,khd->qhd', probs.astype(jnp.float32), values)
        return result.astype(jnp.bfloat16).reshape(PATCH, C)
    attended = lax.map(attend, projected).reshape(point_total, C)
    mixing = jnp.dot(attended, w_out, preferred_element_type=jnp.float32)
    encoded_h = (ordered.astype(jnp.float32) + mixing).astype(jnp.bfloat16)
    encoded = encoded_h[to_hilbert]
    totals = jax.ops.segment_sum(encoded.astype(jnp.float32), parent, POOLED)
    tallies = jax.ops.segment_sum(jnp.ones((point_total,), jnp.float32), parent, POOLED)
    pooled_in = (totals / tallies[:, None]).astype(jnp.bfloat16)
    pooled = jax.nn.gelu(layer_norm(jnp.dot(pooled_in, w_pool, preferred_element_type=jnp.float32))).astype(jnp.bfloat16)
    lifted = jax.nn.gelu(layer_norm(jnp.dot(pooled, w_up, preferred_element_type=jnp.float32))).astype(jnp.bfloat16)
    skipped = jax.nn.gelu(layer_norm(jnp.dot(encoded, w_skip, preferred_element_type=jnp.float32)))
    decoded = (skipped + lifted[parent].astype(jnp.float32)).astype(jnp.bfloat16)
    return (pooled, decoded)
```

```python
import functools

import jax
import jax.numpy as jnp
from jax import lax
from jax.experimental import pallas as pl
from jax.experimental.pallas import tpu as pltpu
from jax.sharding import PartitionSpec as P

ROWS = 512
C = 256
C2 = 512
HEADS = 16
WIDTH = C // HEADS
POOL = ROWS // 2
DEVS = 128
CAP = 8
SLOTS = DEVS * CAP
BLK = 2 * CAP
EXT = POOL + 16
EMPTY = 64.0
QSCALE = WIDTH**-0.5 * 1.4426950408889634
MESH = pl.DeviceIdType.MESH
f32, bf16, i32 = jnp.float32, jnp.bfloat16, jnp.int32


def _offsets():
    far = lambda d: min(d, 4 - d)
    every = [(x, y, c, z) for x in range(4) for y in range(4) for z in range(4) for c in range(2)]
    every.sort(key=lambda o: -(far(o[0]) + far(o[1]) + far(o[3]) + 0.1 * o[2]))
    return [o for o in every if any(o)]


OFFSETS = _offsets()


def dot(a, b):
    return jnp.dot(a, b, preferred_element_type=f32)


def dot_nt(a, b):
    return lax.dot_general(a, b, (((1,), (1,)), ((), ())), preferred_element_type=f32)


def dot_tn(a, b):
    return lax.dot_general(a, b, (((0,), (0,)), ((), ())), preferred_element_type=f32)


def iota(shape, dim):
    return lax.broadcasted_iota(i32, shape, dim)


def onehot(cond):
    return jnp.where(cond, 1.0, 0.0).astype(bf16)


def layer_norm(v):
    center = v - jnp.mean(v, axis=-1, keepdims=True)
    spread = jnp.mean(center * center, axis=-1, keepdims=True)
    return center * lax.rsqrt(spread + 1e-5)


def gelu(v):
    return 0.5 * v * (1.0 + jnp.tanh(0.7978845608028654 * (v + 0.044715 * (v * v * v))))


def to_blocks(v):
    v = v.reshape(DEVS, CAP, C)
    return jnp.concatenate([v[:, :, :128], v[:, :, 128:]], axis=1).reshape(DEVS * BLK, 128)


def from_blocks(b):
    v = b.astype(f32).reshape(DEVS, BLK, 128)
    return jnp.concatenate([v[:, :CAP], v[:, CAP:]], axis=2).reshape(SLOTS, C)


def kernel(
    pt_ref, th_ref, par_ref, wqkv_ref, wout_ref, wpool_ref, wup_ref, wskip_ref,
    pooled_ref, dec_ref,
    out1, in1, out2, in2, bkt_t, comp_t, wq_t, wv_t, nrm, qtm, vta, keys, s_a, s_b, att, tot, tal, e_out, e_in,
    send1, recv1, loc1, send2, recv2, loc2, psend, precv, esend, erecv,
):
    pts, mdl = lax.axis_index("pts"), lax.axis_index("mdl")
    me = pts * 4 + mdl
    core, yy, xx = pts % 2, (pts // 2) % 4, pts // 8
    at_x = [((xx + d) % 4) * 8 for d in range(4)]
    at_y = [((yy + d) % 4) * 2 for d in range(4)]
    at_c = [(core + d) % 2 for d in range(2)]
    at_z = [(mdl + d) % 4 for d in range(4)]

    def place(o):
        return at_x[o[0]] + at_y[o[1]] + at_c[o[2]], at_z[o[3]]

    def block(line):
        return pl.ds(pl.multiple_of(line * BLK, BLK), BLK)

    barrier = pltpu.get_barrier_semaphore()
    for o in OFFSETS:
        pl.semaphore_signal(barrier, inc=1, device_id=place(o), device_id_type=MESH)

    half = th_ref[...] >> 9
    target = (half >> 3) * 8 + (half & 1) * 4 + ((half >> 1) & 3)
    match = jnp.where(iota((DEVS, ROWS), 0) == target, 1.0, 0.0)
    upper = onehot(iota((ROWS, ROWS), 0) < iota((ROWS, ROWS), 1))
    earlier = dot(match.astype(bf16), upper)
    rank = jnp.sum(match * earlier, axis=0, keepdims=True)
    slot = target * CAP + rank.astype(i32)
    bucket = jnp.where(iota((SLOTS, ROWS), 0) == slot, 1.0, 0.0)
    taken = jnp.sum(bucket, axis=1, keepdims=True)
    filled = dot(bucket.astype(bf16), pt_ref[...])
    lane = iota((1, C), 1)
    filled = filled + jnp.where(lane < 128, (1.0 - taken) * EMPTY, 0.0)
    out1[...] = to_blocks(filled).astype(bf16)

    pl.semaphore_wait(barrier, DEVS - 1)

    def exchange(src, dst, send, recv, loc):
        own = pltpu.make_async_copy(src.at[block(me)], dst.at[block(me)], loc)
        for o in OFFSETS:
            p, m = place(o)
            pltpu.make_async_remote_copy(
                src_ref=src.at[block(p * 4 + m)],
                dst_ref=dst.at[block(me)],
                send_sem=send,
                recv_sem=recv,
                device_id=(p, m),
                device_id_type=MESH,
            ).start()
        own.start()

    def finish(src, dst, send, recv, loc):
        most = pl.ds(0, (DEVS - 1) * BLK)
        pltpu.make_async_copy(src.at[block(0)], dst.at[block(0)], loc).wait()
        pltpu.make_async_copy(src.at[most], src.at[most], send).wait()
        pltpu.make_async_copy(dst.at[most], dst.at[most], recv).wait()

    exchange(out1, in1, send1, recv1, loc1)

    slot_cols = jnp.transpose(jnp.broadcast_to(slot.astype(f32), (128, ROWS)))
    lanes = iota((1, 128), 1).astype(f32)
    for k in range(SLOTS // 128):
        bkt_t[:, k * 128 : (k + 1) * 128] = onehot(slot_cols == lanes + k * 128.0)
    wq_t[...] = jnp.transpose(wqkv_ref[:, :C])
    wv_t[...] = jnp.transpose(wqkv_ref[:, 2 * C :])
    qtm[...] = jnp.zeros_like(qtm)
    for h in range(HEADS):
        vta[32 * h + 16 : 32 * h + 32] = jnp.ones((16, 2 * ROWS), bf16)
    lower = onehot(iota((SLOTS, SLOTS), 1) < iota((SLOTS, SLOTS), 0))

    finish(out1, in1, send1, recv1, loc1)

    arrived = from_blocks(in1[...])
    valid = jnp.broadcast_to(jnp.where(arrived[:, :1] < 32.0, 1.0, 0.0), (SLOTS, 128))
    place_of = jnp.where(valid > 0.0, dot(lower, valid.astype(bf16)), -1.0)
    for k in range(ROWS // 128):
        comp_t[:, k * 128 : (k + 1) * 128] = onehot(place_of == lanes + k * 128.0)
    place_row = jnp.transpose(place_of)[:1].astype(i32)
    comp = onehot(iota((ROWS, SLOTS), 0) == place_row)
    ordered = dot(comp, arrived.astype(bf16))
    normed = layer_norm(ordered).astype(bf16)
    nrm[0] = normed

    swap = pltpu.make_async_remote_copy(
        src_ref=nrm.at[0], dst_ref=nrm.at[1], send_sem=psend, recv_sem=precv,
        device_id=(at_x[0] + at_y[0] + at_c[1], mdl), device_id_type=MESH,
    )
    swap.start()

    queries = (dot_nt(wq_t[...], normed) * QSCALE).astype(bf16)
    for h in range(HEADS):
        low = h * 128 + (16 * h) % 128
        qtm[low : low + 16] = queries[16 * h : 16 * h + 16]

    def project(part, rows):
        keys[part * ROWS : (part + 1) * ROWS] = dot(rows, wqkv_ref[:, C : 2 * C]).astype(bf16)
        values = dot_nt(wv_t[...], rows).astype(bf16)
        for h in range(HEADS):
            vta[32 * h : 32 * h + 16, part * ROWS : (part + 1) * ROWS] = values[16 * h : 16 * h + 16]

    project(0, normed)
    swap.wait()
    project(1, nrm[1])

    def scores(buf, h):
        q = qtm[pl.ds(pl.multiple_of(h * 128, 128), 128)]
        s = dot(keys[:, pl.ds(pl.multiple_of((h // 8) * 128, 128), 128)], q)
        buf[...] = s
        return jnp.max(s, axis=0, keepdims=True)

    def weigh(buf, highest, h):
        p = jnp.exp2(buf[...] - highest).astype(bf16)
        o = dot(vta[pl.ds(pl.multiple_of(h * 32, 32), 32)], p)
        att[pl.ds(pl.multiple_of(h * 16, 16), 16)] = (o[:16] / o[16:17]).astype(bf16)

    def two_heads(i, highest):
        h = 2 * i
        second = scores(s_b, h + 1)
        weigh(s_a, highest, h)
        third = scores(s_a, jnp.minimum(h + 2, HEADS - 1))
        weigh(s_b, second, h + 1)
        return third

    lax.fori_loop(0, HEADS // 2, two_heads, scores(s_a, 0))

    encoded_h = (ordered + dot_tn(att[...], wout_ref[...])).astype(bf16)
    out2[...] = to_blocks(dot(comp_t[...], encoded_h)).astype(bf16)
    exchange(out2, in2, send2, recv2, loc2)

    own_row = par_ref[...] - me * POOL
    member = onehot(iota((EXT, ROWS), 0) == jnp.where(own_row < 0, POOL, own_row))
    counts = dot(member, jnp.ones((ROWS, 128), bf16))
    own_cols = jnp.transpose(jnp.broadcast_to(own_row.astype(f32), (128, ROWS)))
    member_t = jnp.concatenate([onehot(own_cols == lanes + k * 128.0) for k in range(POOL // 128)], axis=1)
    spilled = jnp.where(own_cols < 0.0, 1.0, 0.0)

    finish(out2, in2, send2, recv2, loc2)

    encoded = dot(bkt_t[...], from_blocks(in2[...]).astype(bf16)).astype(bf16)
    totals = dot(member, encoded)
    tot[...] = totals
    tal[...] = counts
    e_out[0, :, :C] = totals[POOL : POOL + 8]
    e_out[0, :, C:] = counts[POOL : POOL + 8]
    e_out[1, :, :C] = totals[POOL - 8 : POOL]
    e_out[1, :, C:] = counts[POOL - 8 : POOL]

    def edge(k, line):
        return pltpu.make_async_remote_copy(
            src_ref=e_out.at[k], dst_ref=e_in.at[k], send_sem=esend.at[k], recv_sem=erecv.at[k],
            device_id=(line // 4, line % 4), device_id_type=MESH,
        )

    to_previous = edge(0, (me + DEVS - 1) % DEVS)
    to_next = edge(1, (me + 1) % DEVS)
    to_previous.start()
    to_next.start()

    skipped = gelu(layer_norm(dot(encoded, wskip_ref[...])))

    to_previous.wait()
    to_next.wait()
    tot[POOL - 1 : POOL] += e_in[0, :1, :C]
    tal[POOL - 1 : POOL] += e_in[0, :1, C:]
    tot[POOL : POOL + 1] += e_in[1, 7:8, :C]
    tal[POOL : POOL + 1] += e_in[1, 7:8, C:]
    tallies = jnp.maximum(tal[...], 1.0)
    pooled_in = (tot[...] / jnp.concatenate([tallies, tallies], axis=1)).astype(bf16)
    pooled = gelu(layer_norm(dot(pooled_in, wpool_ref[...]))).astype(bf16)
    pooled_ref[...] = pooled[:POOL]
    lifted = gelu(layer_norm(dot(pooled, wup_ref[...]))).astype(bf16)
    picked = dot(member_t, lifted[:POOL])
    carried = lifted[POOL : POOL + 16].astype(f32)[:1]
    picked = picked + jnp.concatenate([spilled, spilled], axis=1) * carried
    dec_ref[...] = (skipped + picked).astype(bf16)


def on_device(points, to_hilbert, parent, w_qkv, w_out, w_pool, w_up, w_skip):
    vmem = pl.BlockSpec(memory_space=pltpu.VMEM)
    dma = pltpu.SemaphoreType.DMA
    return pl.pallas_call(
        kernel,
        out_shape=(
            jax.ShapeDtypeStruct((POOL, C2), bf16),
            jax.ShapeDtypeStruct((ROWS, C), bf16),
        ),
        in_specs=[vmem] * 8,
        out_specs=(vmem, vmem),
        scratch_shapes=[
            pltpu.VMEM((DEVS * BLK, 128), bf16),
            pltpu.VMEM((DEVS * BLK, 128), bf16),
            pltpu.VMEM((DEVS * BLK, 128), bf16),
            pltpu.VMEM((DEVS * BLK, 128), bf16),
            pltpu.VMEM((ROWS, SLOTS), bf16),
            pltpu.VMEM((SLOTS, ROWS), bf16),
            pltpu.VMEM((C, C), bf16),
            pltpu.VMEM((C, C), bf16),
            pltpu.VMEM((2, ROWS, C), bf16),
            pltpu.VMEM((HEADS * 128, ROWS), bf16),
            pltpu.VMEM((HEADS * 32, 2 * ROWS), bf16),
            pltpu.VMEM((2 * ROWS, C), bf16),
            pltpu.VMEM((2 * ROWS, ROWS), f32),
            pltpu.VMEM((2 * ROWS, ROWS), f32),
            pltpu.VMEM((C, ROWS), bf16),
            pltpu.VMEM((EXT, C), f32),
            pltpu.VMEM((EXT, 128), f32),
            pltpu.VMEM((2, 8, C + 128), f32),
            pltpu.VMEM((2, 8, C + 128), f32),
            dma, dma, dma, dma, dma, dma, dma, dma, dma((2,)), dma((2,)),
        ],
        compiler_params=pltpu.CompilerParams(
            collective_id=0, has_side_effects=True, vmem_limit_bytes=48 * 1024 * 1024
        ),
    )(points, to_hilbert.reshape(1, ROWS), parent.reshape(1, ROWS), w_qkv, w_out, w_pool, w_up, w_skip)


def solution(mesh):
    rows = P(("pts", "mdl"), None)
    flat = P(("pts", "mdl"))
    return jax.shard_map(
        on_device,
        mesh=mesh,
        in_specs=(rows, flat, flat, P(), P(), P(), P(), P()),
        out_specs=(rows, rows),
        check_vma=False,
    )
```

```python
import functools

import jax
import jax.numpy as jnp
from jax import lax
from jax.experimental import pallas as pl
from jax.experimental.pallas import tpu as pltpu
from jax.sharding import PartitionSpec as P

ROWS = 512
C = 256
C2 = 512
HEADS = 16
WIDTH = C // HEADS
POOL = ROWS // 2
DEVS = 128
CAP = 8
SLOTS = DEVS * CAP
BLK = 2 * CAP
EMPTY = 64.0
QSCALE = WIDTH**-0.5 * 1.4426950408889634
MESH = pl.DeviceIdType.MESH
f32, bf16, i32 = jnp.float32, jnp.bfloat16, jnp.int32


def _offsets():
    far = lambda d: min(d, 4 - d)
    every = [(x, y, c, z) for x in range(4) for y in range(4) for z in range(4) for c in range(2)]
    every.sort(key=lambda o: -(far(o[0]) + far(o[1]) + far(o[3]) + 0.1 * o[2]))
    return [o for o in every if any(o)]


OFFSETS = _offsets()


def dot(a, b):
    return jnp.dot(a, b, preferred_element_type=f32)


def dot_nt(a, b):
    return lax.dot_general(a, b, (((1,), (1,)), ((), ())), preferred_element_type=f32)


def dot_tn(a, b):
    return lax.dot_general(a, b, (((0,), (0,)), ((), ())), preferred_element_type=f32)


def iota(shape, dim):
    return lax.broadcasted_iota(i32, shape, dim)


def onehot(cond):
    return jnp.where(cond, 1.0, 0.0).astype(bf16)


def layer_norm(v):
    center = v - jnp.mean(v, axis=-1, keepdims=True)
    spread = jnp.mean(center * center, axis=-1, keepdims=True)
    return center * lax.rsqrt(spread + 1e-5)


def gelu(v):
    return 0.5 * v * (1.0 + jnp.tanh(0.7978845608028654 * (v + 0.044715 * (v * v * v))))


def to_blocks(v):
    v = v.reshape(DEVS, CAP, C)
    return jnp.concatenate([v[:, :, :128], v[:, :, 128:]], axis=1).reshape(DEVS * BLK, 128)


def from_blocks(b):
    v = b.astype(f32).reshape(DEVS, BLK, 128)
    return jnp.concatenate([v[:, :CAP], v[:, CAP:]], axis=2).reshape(SLOTS, C)


def kernel(
    *refs,
):
    (given, (pooled_ref, dec_ref), held, rest) = refs[:8], refs[8:10], refs[10:18], refs[18:]
    pt_ref, th_ref, par_ref, wqkv_ref, wout_ref, wpool_ref, wup_ref, wskip_ref = held
    (
    out1, in1, out2, in2, bkt_t, comp_t, wq_t, wv_t, nrm, qtm, vta, keys, s_a, s_b, att, e_out, e_in,
    send1, recv1, loc1, send2, recv2, loc2, psend, precv, esend, erecv, fetched,
    ) = rest
    loads = [pltpu.make_async_copy(given[i], held[i], fetched.at[i]) for i in range(8)]
    for i in (1, 0, 2, 3, 4, 7, 5, 6):
        loads[i].start()
    pts, mdl = lax.axis_index("pts"), lax.axis_index("mdl")
    me = pts * 4 + mdl
    core, yy, xx = pts % 2, (pts // 2) % 4, pts // 8
    at_x = [((xx + d) % 4) * 8 for d in range(4)]
    at_y = [((yy + d) % 4) * 2 for d in range(4)]
    at_c = [(core + d) % 2 for d in range(2)]
    at_z = [(mdl + d) % 4 for d in range(4)]

    def place(o):
        return at_x[o[0]] + at_y[o[1]] + at_c[o[2]], at_z[o[3]]

    def block(line):
        return pl.ds(pl.multiple_of(line * BLK, BLK), BLK)

    barrier = pltpu.get_barrier_semaphore()
    for o in OFFSETS:
        pl.semaphore_signal(barrier, inc=1, device_id=place(o), device_id_type=MESH)

    loads[1].wait()
    half = th_ref[...] >> 9
    target = (half >> 3) * 8 + (half & 1) * 4 + ((half >> 1) & 3)
    match = jnp.where(iota((DEVS, ROWS), 0) == target, 1.0, 0.0)
    upper = onehot(iota((ROWS, ROWS), 0) < iota((ROWS, ROWS), 1))
    earlier = dot(match.astype(bf16), upper)
    rank = jnp.sum(match * earlier, axis=0, keepdims=True)
    slot = target * CAP + rank.astype(i32)
    bucket = jnp.where(iota((SLOTS, ROWS), 0) == slot, 1.0, 0.0)
    taken = jnp.sum(bucket, axis=1, keepdims=True)
    loads[0].wait()
    normed = layer_norm(pt_ref[...].astype(f32)).astype(bf16)
    filled = dot(bucket.astype(bf16), normed)
    lane = iota((1, C), 1)
    filled = filled + jnp.where(lane < 128, (1.0 - taken) * EMPTY, 0.0)
    out1[...] = to_blocks(filled).astype(bf16)

    pl.semaphore_wait(barrier, DEVS - 1)

    def exchange(src, dst, send, recv, loc):
        own = pltpu.make_async_copy(src.at[block(me)], dst.at[block(me)], loc)
        for o in OFFSETS:
            p, m = place(o)
            pltpu.make_async_remote_copy(
                src_ref=src.at[block(p * 4 + m)],
                dst_ref=dst.at[block(me)],
                send_sem=send,
                recv_sem=recv,
                device_id=(p, m),
                device_id_type=MESH,
            ).start()
        own.start()

    def finish(src, dst, send, recv, loc):
        most = pl.ds(0, (DEVS - 1) * BLK)
        pltpu.make_async_copy(src.at[block(0)], dst.at[block(0)], loc).wait()
        pltpu.make_async_copy(src.at[most], src.at[most], send).wait()
        pltpu.make_async_copy(dst.at[most], dst.at[most], recv).wait()

    exchange(out1, in1, send1, recv1, loc1)

    slot_cols = jnp.transpose(jnp.broadcast_to(slot.astype(f32), (128, ROWS)))
    lanes = iota((1, 128), 1).astype(f32)
    for k in range(SLOTS // 128):
        bkt_t[:, k * 128 : (k + 1) * 128] = onehot(slot_cols == lanes + k * 128.0)
    for i in range(2, 8):
        loads[i].wait()
    wq_t[...] = jnp.transpose(wqkv_ref[:, :C])
    wv_t[...] = jnp.transpose(wqkv_ref[:, 2 * C :])
    qtm[...] = jnp.zeros_like(qtm)
    for h in range(HEADS):
        vta[32 * h + 16 : 32 * h + 32] = jnp.ones((16, 2 * ROWS), bf16)
    sublane = iota((DEVS, CAP, 128), 1).astype(f32)
    pick = jnp.where(iota((16, 128), 1) == 0, 32.0, jnp.where(iota((16, 128), 1) == 64, 1.0, 0.0)).astype(bf16)

    finish(out1, in1, send1, recv1, loc1)

    halves = in1[...].astype(f32).reshape(DEVS, BLK, 128)
    valid = jnp.where(halves[:, :CAP] < 32.0, 1.0, 0.0)
    base = jnp.sum(valid, axis=1, keepdims=True)
    step = 1
    while step < DEVS:
        base = base + jnp.concatenate([jnp.zeros((step, 1, 128), f32), base[:-step]], axis=0)
        step *= 2
    base = base - jnp.sum(valid, axis=1, keepdims=True)
    place_of = jnp.where(valid > 0.0, base + sublane, -1.0).reshape(SLOTS, 128)
    high = jnp.floor(place_of * (1.0 / 32.0))
    digits = jnp.where(iota((SLOTS, 128), 1) < 64, high, place_of - 32.0 * high).astype(bf16)
    place_row = dot_nt(pick, digits)[:1].astype(i32)
    comp = onehot(iota((ROWS, SLOTS), 0) == place_row)
    arrived = jnp.concatenate([halves[:, :CAP], halves[:, CAP:]], axis=2).reshape(SLOTS, C).astype(bf16)
    normed = dot(comp, arrived).astype(bf16)
    nrm[0] = normed

    swap = pltpu.make_async_remote_copy(
        src_ref=nrm.at[0], dst_ref=nrm.at[1], send_sem=psend, recv_sem=precv,
        device_id=(at_x[0] + at_y[0] + at_c[1], mdl), device_id_type=MESH,
    )
    swap.start()

    for k in range(ROWS // 128):
        comp_t[:, k * 128 : (k + 1) * 128] = onehot(place_of == lanes + k * 128.0)
    queries = (dot_nt(wq_t[...], normed) * QSCALE).astype(bf16)
    for h in range(HEADS):
        low = h * 128 + (16 * h) % 128
        qtm[low : low + 16] = queries[16 * h : 16 * h + 16]

    def project(part, rows):
        keys[part * ROWS : (part + 1) * ROWS] = dot(rows, wqkv_ref[:, C : 2 * C]).astype(bf16)
        values = dot_nt(wv_t[...], rows).astype(bf16)
        for h in range(HEADS):
            vta[32 * h : 32 * h + 16, part * ROWS : (part + 1) * ROWS] = values[16 * h : 16 * h + 16]

    project(0, normed)
    swap.wait()
    project(1, nrm[1])

    def scores(buf, h):
        q = qtm[pl.ds(pl.multiple_of(h * 128, 128), 128)]
        s = dot(keys[:, pl.ds(pl.multiple_of((h // 8) * 128, 128), 128)], q)
        buf[...] = s
        return jnp.max(s, axis=0, keepdims=True)

    def weigh(buf, highest, h):
        p = jnp.exp2(buf[...] - highest).astype(bf16)
        o = dot(vta[pl.ds(pl.multiple_of(h * 32, 32), 32)], p)
        att[pl.ds(pl.multiple_of(h * 16, 16), 16)] = (o[:16] / o[16:17]).astype(bf16)

    def two_heads(i, highest):
        h = 2 * i
        second = scores(s_b, h + 1)
        weigh(s_a, highest, h)
        third = scores(s_a, jnp.minimum(h + 2, HEADS - 1))
        weigh(s_b, second, h + 1)
        return third

    lax.fori_loop(0, HEADS // 2, two_heads, scores(s_a, 0))

    attended = jnp.transpose(att[...])
    out2[...] = to_blocks(dot(comp_t[...], attended)).astype(bf16)
    exchange(out2, in2, send2, recv2, loc2)

    own_row = par_ref[...] - me * POOL
    member = onehot(iota((POOL, ROWS), 0) == own_row)
    ones = jnp.ones((ROWS, 128), bf16)
    counts = jnp.maximum(dot(member, ones), 1.0)
    edge_member = onehot(jnp.where(iota((16, ROWS), 0) < 8, -1, POOL - 1) == own_row)
    edge_counts = dot(edge_member, ones)
    own_cols = jnp.transpose(jnp.broadcast_to(own_row.astype(f32), (128, ROWS)))
    inner_t = jnp.concatenate(
        [onehot(jnp.where(own_cols == POOL - 1.0, -1.0, own_cols) == lanes + k * 128.0) for k in range(POOL // 128)],
        axis=1,
    )
    last_cols = jnp.where(own_cols == POOL - 1.0, 1.0, 0.0)
    spilled_cols = jnp.where(own_cols < 0.0, 1.0, 0.0)
    for k in range(2):
        e_out[k, :, C:] = edge_counts[8 * k : 8 * k + 8]

    finish(out2, in2, send2, recv2, loc2)

    attended = dot(bkt_t[...], from_blocks(in2[...]).astype(bf16)).astype(bf16)
    encoded = (pt_ref[...].astype(f32) + dot(attended, wout_ref[...])).astype(bf16)
    edge_sums = dot(edge_member, encoded)
    for k in range(2):
        e_out[k, :, :C] = edge_sums[8 * k : 8 * k + 8]

    def edge(k, line):
        return pltpu.make_async_remote_copy(
            src_ref=e_out.at[k], dst_ref=e_in.at[k], send_sem=esend.at[k], recv_sem=erecv.at[k],
            device_id=(line // 4, line % 4), device_id_type=MESH,
        )

    to_previous = edge(0, (me + DEVS - 1) % DEVS)
    to_next = edge(1, (me + 1) % DEVS)
    to_previous.start()
    to_next.start()

    def pool(sums, tallies):
        mean = sums / jnp.concatenate([tallies, tallies], axis=1)
        return gelu(layer_norm(dot(mean.astype(bf16), wpool_ref[...]))).astype(bf16)

    def lift(rows):
        return gelu(layer_norm(dot(rows, wup_ref[...]))).astype(bf16)

    pooled = pool(dot(member, encoded), counts)
    pooled_ref[...] = pooled
    skipped = gelu(layer_norm(dot(encoded, wskip_ref[...])))
    partial = skipped + dot(inner_t, lift(pooled))

    to_previous.wait()
    to_next.wait()
    shared = jnp.concatenate([e_out[1] + e_in[0], e_in[1] + e_out[0]], axis=0)
    shared_pooled = pool(shared[:, :C], jnp.maximum(shared[:, C:], 1.0))
    pooled_ref[POOL - 16 :] = jnp.where(iota((16, C2), 0) == 15, shared_pooled[:1], pooled[POOL - 16 :])
    shared_lifted = lift(shared_pooled).astype(f32)
    both = lambda v: jnp.concatenate([v, v], axis=1)
    picked = both(last_cols) * shared_lifted[:1] + both(spilled_cols) * shared_lifted[8:9]
    dec_ref[...] = (partial + picked).astype(bf16)


def hand_out(pooled_ref, dec_ref, pooled_out, dec_out, sems):
    first = pltpu.make_async_copy(dec_ref, dec_out, sems.at[0])
    second = pltpu.make_async_copy(pooled_ref, pooled_out, sems.at[1])
    first.start()
    second.start()
    first.wait()
    second.wait()


def on_device(points, to_hilbert, parent, w_qkv, w_out, w_pool, w_up, w_skip):
    given = (points, to_hilbert.reshape(1, ROWS), parent.reshape(1, ROWS), w_qkv, w_out, w_pool, w_up, w_skip)
    vmem = pl.BlockSpec(memory_space=pltpu.VMEM)
    dma = pltpu.SemaphoreType.DMA
    held = [pltpu.with_memory_space_constraint(v, pltpu.HBM) for v in given]
    results = pl.pallas_call(
        kernel,
        out_shape=(pltpu.VMEM((POOL, C2), bf16), pltpu.VMEM((ROWS, C), bf16)),
        in_specs=[pl.BlockSpec(memory_space=pltpu.HBM)] * 8,
        out_specs=(vmem, vmem),
        scratch_shapes=[
            pltpu.VMEM((ROWS, C), bf16),
            pltpu.VMEM((1, ROWS), i32),
            pltpu.VMEM((1, ROWS), i32),
            pltpu.VMEM((C, 3 * C), bf16),
            pltpu.VMEM((C, C), bf16),
            pltpu.VMEM((C, C2), bf16),
            pltpu.VMEM((C2, C), bf16),
            pltpu.VMEM((C, C), bf16),
            pltpu.VMEM((DEVS * BLK, 128), bf16),
            pltpu.VMEM((DEVS * BLK, 128), bf16),
            pltpu.VMEM((DEVS * BLK, 128), bf16),
            pltpu.VMEM((DEVS * BLK, 128), bf16),
            pltpu.VMEM((ROWS, SLOTS), bf16),
            pltpu.VMEM((SLOTS, ROWS), bf16),
            pltpu.VMEM((C, C), bf16),
            pltpu.VMEM((C, C), bf16),
            pltpu.VMEM((2, ROWS, C), bf16),
            pltpu.VMEM((HEADS * 128, ROWS), bf16),
            pltpu.VMEM((HEADS * 32, 2 * ROWS), bf16),
            pltpu.VMEM((2 * ROWS, C), bf16),
            pltpu.VMEM((2 * ROWS, ROWS), f32),
            pltpu.VMEM((2 * ROWS, ROWS), f32),
            pltpu.VMEM((C, ROWS), bf16),
            pltpu.VMEM((2, 8, C + 128), f32),
            pltpu.VMEM((2, 8, C + 128), f32),
            dma, dma, dma, dma, dma, dma, dma, dma, dma((2,)), dma((2,)), dma((8,)),
        ],
        compiler_params=pltpu.CompilerParams(
            collective_id=0, has_side_effects=True, vmem_limit_bytes=48 * 1024 * 1024
        ),
    )(*held)
    anywhere = pl.BlockSpec(memory_space=pl.ANY)
    return pl.pallas_call(
        hand_out,
        out_shape=(jax.ShapeDtypeStruct((POOL, C2), bf16), jax.ShapeDtypeStruct((ROWS, C), bf16)),
        in_specs=[anywhere, anywhere],
        out_specs=(anywhere, anywhere),
        scratch_shapes=[dma((2,))],
    )(*results)


def solution(mesh):
    rows = P(("pts", "mdl"), None)
    flat = P(("pts", "mdl"))
    return jax.shard_map(
        on_device,
        mesh=mesh,
        in_specs=(rows, flat, flat, P(), P(), P(), P(), P()),
        out_specs=(rows, rows),
        check_vma=False,
    )
```

```python
import functools

import jax
import jax.numpy as jnp
from jax import lax
from jax.experimental import pallas as pl
from jax.experimental.pallas import tpu as pltpu
from jax.sharding import PartitionSpec as P

ROWS = 512
C = 256
C2 = 512
HEADS = 16
WIDTH = C // HEADS
POOL = ROWS // 2
DEVS = 128
CAP = 8
SLOTS = DEVS * CAP
BLK = 2 * CAP
EMPTY = 64.0
QSCALE = WIDTH**-0.5 * 1.4426950408889634
MESH = pl.DeviceIdType.MESH
f32, bf16, i32 = jnp.float32, jnp.bfloat16, jnp.int32


def _offsets():
    far = lambda d: min(d, 4 - d)
    every = [(x, y, c, z) for x in range(4) for y in range(4) for z in range(4) for c in range(2)]
    every.sort(key=lambda o: -(far(o[0]) + far(o[1]) + far(o[3]) + 0.1 * o[2]))
    return [o for o in every if any(o)]


OFFSETS = _offsets()


def dot(a, b):
    return jnp.dot(a, b, preferred_element_type=f32)


def dot_nt(a, b):
    return lax.dot_general(a, b, (((1,), (1,)), ((), ())), preferred_element_type=f32)


def dot_tn(a, b):
    return lax.dot_general(a, b, (((0,), (0,)), ((), ())), preferred_element_type=f32)


def iota(shape, dim):
    return lax.broadcasted_iota(i32, shape, dim)


def onehot(cond):
    return jnp.where(cond, 1.0, 0.0).astype(bf16)


def layer_norm(v):
    center = v - jnp.mean(v, axis=-1, keepdims=True)
    spread = jnp.mean(center * center, axis=-1, keepdims=True)
    return center * lax.rsqrt(spread + 1e-5)


def gelu(v):
    return 0.5 * v * (1.0 + jnp.tanh(0.7978845608028654 * (v + 0.044715 * (v * v * v))))


def to_blocks(v):
    v = v.reshape(DEVS, CAP, C)
    return jnp.concatenate([v[:, :, :128], v[:, :, 128:]], axis=1).reshape(DEVS * BLK, 128)


def kernel(
    *refs,
):
    (given, (pooled_ref, dec_ref), held, rest) = refs[:8], refs[8:10], refs[10:18], refs[18:]
    pt_ref, th_ref, par_ref, wqkv_ref, wout_ref, wpool_ref, wup_ref, wskip_ref = held
    (
    out1, in1, out2, in2, bkt_t, comp_t, wq_t, wv_t, nrm, qtm, vta, keys, s_a, s_b, att, e_out, e_in,
    send1, recv1, loc1, send2, recv2, loc2, psend, precv, esend, erecv, fetched,
    ) = rest
    loads = [pltpu.make_async_copy(given[i], held[i], fetched.at[i]) for i in range(8)]
    pts, mdl = lax.axis_index("pts"), lax.axis_index("mdl")
    me = pts * 4 + mdl
    core, yy, xx = pts % 2, (pts // 2) % 4, pts // 8
    at_x = [((xx + d) % 4) * 8 for d in range(4)]
    at_y = [((yy + d) % 4) * 2 for d in range(4)]
    at_c = [(core + d) % 2 for d in range(2)]
    at_z = [(mdl + d) % 4 for d in range(4)]

    def place(o):
        return at_x[o[0]] + at_y[o[1]] + at_c[o[2]], at_z[o[3]]

    def block(line):
        return pl.ds(pl.multiple_of(line * BLK, BLK), BLK)

    barrier = pltpu.get_barrier_semaphore()
    for k, o in enumerate(OFFSETS):
        pl.semaphore_signal(barrier, inc=1, device_id=place(o), device_id_type=MESH)
        if k == 15:
            for i in (1, 0, 2, 3, 4, 7, 5, 6):
                loads[i].start()

    loads[1].wait()
    half = th_ref[...] >> 9
    target = (half >> 3) * 8 + (half & 1) * 4 + ((half >> 1) & 3)
    match = jnp.where(iota((DEVS, ROWS), 0) == target, 1.0, 0.0)
    upper = onehot(iota((ROWS, ROWS), 0) < iota((ROWS, ROWS), 1))
    earlier = dot(match.astype(bf16), upper)
    rank = jnp.sum(match * earlier, axis=0, keepdims=True)
    slot = target * CAP + rank.astype(i32)
    bucket = jnp.where(iota((SLOTS, ROWS), 0) == slot, 1.0, 0.0)
    taken = jnp.sum(bucket, axis=1, keepdims=True)
    loads[0].wait()
    normed = layer_norm(pt_ref[...].astype(f32)).astype(bf16)
    filled = dot(bucket.astype(bf16), normed)
    lane = iota((1, C), 1)
    filled = filled + jnp.where(lane < 128, (1.0 - taken) * EMPTY, 0.0)
    out1[...] = to_blocks(filled).astype(bf16)

    pl.semaphore_wait(barrier, DEVS - 1)

    def exchange(src, dst, send, recv, loc):
        own = pltpu.make_async_copy(src.at[block(me)], dst.at[block(me)], loc)
        for o in OFFSETS:
            p, m = place(o)
            pltpu.make_async_remote_copy(
                src_ref=src.at[block(p * 4 + m)],
                dst_ref=dst.at[block(me)],
                send_sem=send,
                recv_sem=recv,
                device_id=(p, m),
                device_id_type=MESH,
            ).start()
        own.start()

    def finish(src, dst, send, recv, loc):
        most = pl.ds(0, (DEVS - 1) * BLK)
        pltpu.make_async_copy(src.at[block(0)], dst.at[block(0)], loc).wait()
        pltpu.make_async_copy(src.at[most], src.at[most], send).wait()
        pltpu.make_async_copy(dst.at[most], dst.at[most], recv).wait()

    exchange(out1, in1, send1, recv1, loc1)

    slot_cols = jnp.transpose(jnp.broadcast_to(slot.astype(f32), (128, ROWS)))
    lanes = iota((1, 128), 1).astype(f32)
    for k in range(SLOTS // 128):
        bkt_t[:, k * 128 : (k + 1) * 128] = onehot(slot_cols == lanes + k * 128.0)
    for i in range(2, 8):
        loads[i].wait()
    wq_t[...] = jnp.transpose(wqkv_ref[:, :C])
    wv_t[...] = jnp.transpose(wqkv_ref[:, 2 * C :])
    qtm[...] = jnp.zeros_like(qtm)
    sublane = iota((DEVS, CAP, 128), 1).astype(f32)
    pick = jnp.where(iota((16, 128), 1) == 0, 32.0, jnp.where(iota((16, 128), 1) == 64, 1.0, 0.0)).astype(bf16)

    finish(out1, in1, send1, recv1, loc1)

    halves = in1[...].astype(f32).reshape(DEVS, BLK, 128)
    valid = jnp.where(halves[:, :CAP] < 32.0, 1.0, 0.0)
    base = jnp.sum(valid, axis=1, keepdims=True)
    step = 1
    while step < DEVS:
        base = base + jnp.concatenate([jnp.zeros((step, 1, 128), f32), base[:-step]], axis=0)
        step *= 2
    base = base - jnp.sum(valid, axis=1, keepdims=True)
    place_of = jnp.where(valid > 0.0, base + sublane, -1.0).reshape(SLOTS, 128)
    high = jnp.floor(place_of * (1.0 / 32.0))
    digits = jnp.where(iota((SLOTS, 128), 1) < 64, high, place_of - 32.0 * high).astype(bf16)
    place_row = dot_nt(pick, digits)[:1].astype(i32)
    comp = onehot(iota((ROWS, SLOTS), 0) == place_row)
    arrived = jnp.concatenate([halves[:, :CAP], halves[:, CAP:]], axis=2).reshape(SLOTS, C).astype(bf16)
    normed = dot(comp, arrived).astype(bf16)
    nrm[0] = normed

    swap = pltpu.make_async_remote_copy(
        src_ref=nrm.at[0], dst_ref=nrm.at[1], send_sem=psend, recv_sem=precv,
        device_id=(at_x[0] + at_y[0] + at_c[1], mdl), device_id_type=MESH,
    )
    swap.start()

    for k in range(ROWS // 128):
        comp_t[:, k * 128 : (k + 1) * 128] = onehot(place_of == lanes + k * 128.0)
    queries = (dot_nt(wq_t[...], normed) * QSCALE).astype(bf16)
    for h in range(HEADS):
        low = h * 128 + (16 * h) % 128
        qtm[low : low + 16] = queries[16 * h : 16 * h + 16]

    def project(part, rows):
        keys[part * ROWS : (part + 1) * ROWS] = dot(rows, wqkv_ref[:, C : 2 * C]).astype(bf16)
        values = dot_nt(wv_t[...], rows).astype(bf16)
        vta[:, part * ROWS : (part + 1) * ROWS] = values

    project(0, normed)
    swap.wait()
    project(1, nrm[1])

    def scores(buf, h):
        q = qtm[pl.ds(pl.multiple_of(h * 128, 128), 128)]
        s = dot(keys[:, pl.ds(pl.multiple_of((h // 8) * 128, 128), 128)], q)
        buf[...] = s
        return jnp.max(s, axis=0, keepdims=True)

    def weigh(buf, highest, h):
        weights = jnp.exp2(buf[...] - highest)
        total = jnp.sum(weights, axis=0, keepdims=True)
        p = weights.astype(bf16)
        o = dot(vta[pl.ds(pl.multiple_of(h * WIDTH, WIDTH), WIDTH)], p)
        att[pl.ds(pl.multiple_of(h * WIDTH, WIDTH), WIDTH)] = (o / total).astype(bf16)

    def two_heads(i, highest):
        h = 2 * i
        second = scores(s_b, h + 1)
        weigh(s_a, highest, h)
        third = scores(s_a, jnp.minimum(h + 2, HEADS - 1))
        weigh(s_b, second, h + 1)
        return third

    def back(half):
        rows = jnp.transpose(att[half * 128 : (half + 1) * 128])
        out2[half] = dot(comp_t[...], rows).reshape(DEVS, CAP, 128).astype(bf16)
        pltpu.make_async_copy(out2.at[half, me], in2.at[half, me], loc2.at[half]).start()

        def send(o):
            p, m = place(o)
            pltpu.make_async_remote_copy(
                src_ref=out2.at[half, p * 4 + m],
                dst_ref=in2.at[half, me],
                send_sem=send2.at[half],
                recv_sem=recv2.at[half],
                device_id=(p, m),
                device_id_type=MESH,
            ).start()

        return [functools.partial(send, o) for o in OFFSETS]

    def back_wait(half):
        pltpu.make_async_copy(out2.at[half, 0], in2.at[half, 0], loc2.at[half]).wait()
        pltpu.make_async_copy(out2.at[half, : DEVS - 1], out2.at[half, : DEVS - 1], send2.at[half]).wait()
        pltpu.make_async_copy(in2.at[half, : DEVS - 1], in2.at[half, : DEVS - 1], recv2.at[half]).wait()
        return in2[half].astype(f32).reshape(SLOTS, 128).astype(bf16)

    quarter = HEADS // 4
    highest = lax.fori_loop(0, quarter, two_heads, scores(s_a, 0))
    sends = back(0)
    for send in sends:
        send()
    lax.fori_loop(quarter, 2 * quarter, two_heads, highest)
    for send in back(1):
        send()

    own_row = par_ref[...] - me * POOL
    member = onehot(iota((POOL, ROWS), 0) == own_row)
    ones = jnp.ones((ROWS, 128), bf16)
    counts = jnp.maximum(dot(member, ones), 1.0)
    edge_member = onehot(jnp.where(iota((16, ROWS), 0) < 8, -1, POOL - 1) == own_row)
    edge_counts = dot(edge_member, ones)
    own_cols = jnp.transpose(jnp.broadcast_to(own_row.astype(f32), (128, ROWS)))
    inner_t = jnp.concatenate(
        [onehot(jnp.where(own_cols == POOL - 1.0, -1.0, own_cols) == lanes + k * 128.0) for k in range(POOL // 128)],
        axis=1,
    )
    last_cols = jnp.where(own_cols == POOL - 1.0, 1.0, 0.0)
    spilled_cols = jnp.where(own_cols < 0.0, 1.0, 0.0)
    for k in range(2):
        e_out[k, :, C:] = edge_counts[8 * k : 8 * k + 8]

    attended = [dot(bkt_t[...], back_wait(half)).astype(bf16) for half in range(2)]
    attended = jnp.concatenate(attended, axis=1)
    encoded = (pt_ref[...].astype(f32) + dot(attended, wout_ref[...])).astype(bf16)
    edge_sums = dot(edge_member, encoded)
    for k in range(2):
        e_out[k, :, :C] = edge_sums[8 * k : 8 * k + 8]

    def edge(k, line):
        return pltpu.make_async_remote_copy(
            src_ref=e_out.at[k], dst_ref=e_in.at[k], send_sem=esend.at[k], recv_sem=erecv.at[k],
            device_id=(line // 4, line % 4), device_id_type=MESH,
        )

    to_previous = edge(0, (me + DEVS - 1) % DEVS)
    to_next = edge(1, (me + 1) % DEVS)
    to_previous.start()
    to_next.start()

    def pool(sums, tallies):
        mean = sums / jnp.concatenate([tallies, tallies], axis=1)
        return gelu(layer_norm(dot(mean.astype(bf16), wpool_ref[...]))).astype(bf16)

    def lift(rows):
        return gelu(layer_norm(dot(rows, wup_ref[...]))).astype(bf16)

    pooled = pool(dot(member, encoded), counts)
    pooled_ref[...] = pooled
    skipped = gelu(layer_norm(dot(encoded, wskip_ref[...])))
    partial = skipped + dot(inner_t, lift(pooled))

    to_previous.wait()
    to_next.wait()
    shared = jnp.concatenate([e_out[1] + e_in[0], e_in[1] + e_out[0]], axis=0)
    shared_pooled = pool(shared[:, :C], jnp.maximum(shared[:, C:], 1.0))
    pooled_ref[POOL - 16 :] = jnp.where(iota((16, C2), 0) == 15, shared_pooled[:1], pooled[POOL - 16 :])
    shared_lifted = lift(shared_pooled).astype(f32)
    both = lambda v: jnp.concatenate([v, v], axis=1)
    picked = both(last_cols) * shared_lifted[:1] + both(spilled_cols) * shared_lifted[8:9]
    dec_ref[...] = (partial + picked).astype(bf16)


def hand_out(pooled_ref, dec_ref, pooled_out, dec_out, sems):
    first = pltpu.make_async_copy(dec_ref, dec_out, sems.at[0])
    second = pltpu.make_async_copy(pooled_ref, pooled_out, sems.at[1])
    first.start()
    second.start()
    first.wait()
    second.wait()


def on_device(points, to_hilbert, parent, w_qkv, w_out, w_pool, w_up, w_skip):
    given = (points, to_hilbert.reshape(1, ROWS), parent.reshape(1, ROWS), w_qkv, w_out, w_pool, w_up, w_skip)
    vmem = pl.BlockSpec(memory_space=pltpu.VMEM)
    dma = pltpu.SemaphoreType.DMA
    held = [pltpu.with_memory_space_constraint(v, pltpu.HBM) for v in given]
    results = pl.pallas_call(
        kernel,
        out_shape=(pltpu.VMEM((POOL, C2), bf16), pltpu.VMEM((ROWS, C), bf16)),
        in_specs=[pl.BlockSpec(memory_space=pltpu.HBM)] * 8,
        out_specs=(vmem, vmem),
        scratch_shapes=[
            pltpu.VMEM((ROWS, C), bf16),
            pltpu.VMEM((1, ROWS), i32),
            pltpu.VMEM((1, ROWS), i32),
            pltpu.VMEM((C, 3 * C), bf16),
            pltpu.VMEM((C, C), bf16),
            pltpu.VMEM((C, C2), bf16),
            pltpu.VMEM((C2, C), bf16),
            pltpu.VMEM((C, C), bf16),
            pltpu.VMEM((DEVS * BLK, 128), bf16),
            pltpu.VMEM((DEVS * BLK, 128), bf16),
            pltpu.VMEM((2, DEVS, CAP, 128), bf16),
            pltpu.VMEM((2, DEVS, CAP, 128), bf16),
            pltpu.VMEM((ROWS, SLOTS), bf16),
            pltpu.VMEM((SLOTS, ROWS), bf16),
            pltpu.VMEM((C, C), bf16),
            pltpu.VMEM((C, C), bf16),
            pltpu.VMEM((2, ROWS, C), bf16),
            pltpu.VMEM((HEADS * 128, ROWS), bf16),
            pltpu.VMEM((C, 2 * ROWS), bf16),
            pltpu.VMEM((2 * ROWS, C), bf16),
            pltpu.VMEM((2 * ROWS, ROWS), f32),
            pltpu.VMEM((2 * ROWS, ROWS), f32),
            pltpu.VMEM((C, ROWS), bf16),
            pltpu.VMEM((2, 8, C + 128), f32),
            pltpu.VMEM((2, 8, C + 128), f32),
            dma, dma, dma, dma((2,)), dma((2,)), dma((2,)), dma, dma, dma((2,)), dma((2,)), dma((8,)),
        ],
        compiler_params=pltpu.CompilerParams(
            collective_id=0, has_side_effects=True, vmem_limit_bytes=48 * 1024 * 1024
        ),
    )(*held)
    results = [pltpu.with_memory_space_constraint(v, pltpu.VMEM) for v in results]
    anywhere = pl.BlockSpec(memory_space=pl.ANY)
    return pl.pallas_call(
        hand_out,
        out_shape=(jax.ShapeDtypeStruct((POOL, C2), bf16), jax.ShapeDtypeStruct((ROWS, C), bf16)),
        in_specs=[vmem, vmem],
        out_specs=(anywhere, anywhere),
        scratch_shapes=[dma((2,))],
    )(*results)


def solution(mesh):
    rows = P(("pts", "mdl"), None)
    flat = P(("pts", "mdl"))
    return jax.shard_map(
        on_device,
        mesh=mesh,
        in_specs=(rows, flat, flat, P(), P(), P(), P(), P()),
        out_specs=(rows, rows),
        check_vma=False,
    )
```

```python
import functools

import jax
import jax.numpy as jnp
from jax import lax
from jax.experimental import pallas as pl
from jax.experimental.pallas import tpu as pltpu
from jax.sharding import PartitionSpec as P

ROWS = 512
C = 256
C2 = 512
HEADS = 16
WIDTH = C // HEADS
POOL = ROWS // 2
DEVS = 128
CAP = 8
SLOTS = DEVS * CAP
BLK = 2 * CAP
EMPTY = 64.0
QSCALE = WIDTH**-0.5 * 1.4426950408889634
MESH = pl.DeviceIdType.MESH
f32, bf16, i32 = jnp.float32, jnp.bfloat16, jnp.int32


def _offsets():
    far = lambda d: min(d, 4 - d)
    every = [(x, y, c, z) for x in range(4) for y in range(4) for z in range(4) for c in range(2)]
    every.sort(key=lambda o: -(far(o[0]) + far(o[1]) + far(o[3]) + 0.1 * o[2]))
    return [o for o in every if any(o)]


OFFSETS = _offsets()
FIRST = 32
QUERIES = FIRST * CAP


def minus(o):
    return tuple((-v) % (2 if k == 2 else 4) for k, v in enumerate(o))


def dot(a, b):
    return jnp.dot(a, b, preferred_element_type=f32)


def dot_nt(a, b):
    return lax.dot_general(a, b, (((1,), (1,)), ((), ())), preferred_element_type=f32)


def dot_tn(a, b):
    return lax.dot_general(a, b, (((0,), (0,)), ((), ())), preferred_element_type=f32)


def iota(shape, dim):
    return lax.broadcasted_iota(i32, shape, dim)


def onehot(cond):
    return jnp.where(cond, 1.0, 0.0).astype(bf16)


def layer_norm(v):
    center = v - jnp.mean(v, axis=-1, keepdims=True)
    spread = jnp.mean(center * center, axis=-1, keepdims=True)
    return center * lax.rsqrt(spread + 1e-5)


def gelu(v):
    return 0.5 * v * (1.0 + jnp.tanh(0.7978845608028654 * (v + 0.044715 * (v * v * v))))


def to_blocks(v):
    v = v.reshape(DEVS, CAP, C)
    return jnp.concatenate([v[:, :, :128], v[:, :, 128:]], axis=1).reshape(DEVS * BLK, 128)


def kernel(
    *refs,
):
    (given, (pooled_ref, dec_ref), held, rest) = refs[:8], refs[8:10], refs[10:18], refs[18:]
    pt_ref, th_ref, par_ref, wqkv_ref, wout_ref, wpool_ref, wup_ref, wskip_ref = held
    (
    out1, in1, out2, in2, bkt_t, comp_t, wq_t, wv_t, nrm, qtm, vta, keys, s_0, s_1, s_2, s_3, att, part_o, part_l, part_m, e_out, e_in,
    send1, recv1, loc1, send2, recv2, loc2, psend, precv, esend, erecv, fetched,
    ) = rest
    loads = [pltpu.make_async_copy(given[i], held[i], fetched.at[i]) for i in range(8)]
    pts, mdl = lax.axis_index("pts"), lax.axis_index("mdl")
    me = pts * 4 + mdl
    core, yy, xx = pts % 2, (pts // 2) % 4, pts // 8
    at_x = [((xx + d) % 4) * 8 for d in range(4)]
    at_y = [((yy + d) % 4) * 2 for d in range(4)]
    at_c = [(core + d) % 2 for d in range(2)]
    at_z = [(mdl + d) % 4 for d in range(4)]

    def place(o):
        return at_x[o[0]] + at_y[o[1]] + at_c[o[2]], at_z[o[3]]

    def block(line):
        return pl.ds(pl.multiple_of(line * BLK, BLK), BLK)

    barrier = pltpu.get_barrier_semaphore()
    for k, o in enumerate(OFFSETS):
        pl.semaphore_signal(barrier, inc=1, device_id=place(o), device_id_type=MESH)
        if k == 15:
            for i in (1, 0, 2, 3, 4, 7, 5, 6):
                loads[i].start()

    loads[1].wait()
    half = th_ref[...] >> 9
    target = (half >> 3) * 8 + (half & 1) * 4 + ((half >> 1) & 3)
    match = jnp.where(iota((DEVS, ROWS), 0) == target, 1.0, 0.0)
    upper = onehot(iota((ROWS, ROWS), 0) < iota((ROWS, ROWS), 1))
    earlier = dot(match.astype(bf16), upper)
    rank = jnp.sum(match * earlier, axis=0, keepdims=True)
    slot = target * CAP + rank.astype(i32)
    bucket = jnp.where(iota((SLOTS, ROWS), 0) == slot, 1.0, 0.0)
    taken = jnp.sum(bucket, axis=1, keepdims=True)
    loads[0].wait()
    normed = layer_norm(pt_ref[...].astype(f32)).astype(bf16)
    filled = dot(bucket.astype(bf16), normed)
    lane = iota((1, C), 1)
    filled = filled + jnp.where(lane < 128, (1.0 - taken) * EMPTY, 0.0)
    out1[...] = to_blocks(filled).astype(bf16)

    pl.semaphore_wait(barrier, DEVS - 1)

    last = (DEVS - 1) * BLK
    own = pltpu.make_async_copy(out1.at[block(me)], in1.at[pl.ds(last, BLK)], loc1)
    own.start()
    for o in OFFSETS:
        p, m = place(o)
        pltpu.make_async_remote_copy(
            src_ref=out1.at[block(p * 4 + m)],
            dst_ref=in1.at[pl.ds(OFFSETS.index(minus(o)) * BLK, BLK)],
            send_sem=send1,
            recv_sem=recv1,
            device_id=(p, m),
            device_id_type=MESH,
        ).start()

    slot_cols = jnp.transpose(jnp.broadcast_to(slot.astype(f32), (128, ROWS)))
    lanes = iota((1, 128), 1).astype(f32)
    for k in range(SLOTS // 128):
        bkt_t[:, k * 128 : (k + 1) * 128] = onehot(slot_cols == lanes + k * 128.0)
    for i in range(2, 8):
        loads[i].wait()
    wq_t[...] = jnp.transpose(wqkv_ref[:, :C])
    wv_t[...] = jnp.transpose(wqkv_ref[:, 2 * C :])
    qtm[...] = jnp.zeros_like(qtm)
    sublane = iota((DEVS, CAP, 128), 1).astype(f32)
    pick = jnp.where(iota((16, 128), 1) == 0, 32.0, jnp.where(iota((16, 128), 1) == 64, 1.0, 0.0)).astype(bf16)

    own.wait()
    came = in1.at[pl.ds(0, last)]
    pltpu.make_async_copy(came, came, recv1).wait()
    halves = in1[...].astype(f32).reshape(DEVS, BLK, 128)
    valid = jnp.where(halves[:, :CAP] < 32.0, 1.0, 0.0)
    counts = jnp.sum(valid, axis=1, keepdims=True)
    upto = counts
    for step in (1, 2, 4, 8, 16, 32, 64):
        upto = upto + jnp.concatenate([jnp.zeros((step, 1, 128), f32), upto[:-step]], axis=0)
    place_of = jnp.where(valid > 0.0, upto - counts + sublane, -1.0).reshape(SLOTS, 128)
    high = jnp.floor(place_of * (1.0 / 32.0))
    digits = jnp.where(iota((SLOTS, 128), 1) < 64, high, place_of - 32.0 * high).astype(bf16)
    place_row = dot_nt(pick, digits)[:1].astype(i32)
    comp = onehot(iota((ROWS, SLOTS), 0) == place_row)
    arrived = jnp.concatenate([halves[:, :CAP], halves[:, CAP:]], axis=2).reshape(SLOTS, C).astype(bf16)
    normed = dot(comp, arrived).astype(bf16)
    nrm[0] = normed

    swap = pltpu.make_async_remote_copy(
        src_ref=nrm.at[0], dst_ref=nrm.at[1], send_sem=psend, recv_sem=precv,
        device_id=(at_x[0] + at_y[0] + at_c[1], mdl), device_id_type=MESH,
    )
    swap.start()

    for c in range(ROWS // 128):
        comp_t[:, c * 128 : (c + 1) * 128] = onehot(place_of == lanes + c * 128.0)
    queries = (dot_nt(wq_t[...], normed) * QSCALE).astype(bf16)
    for h in range(HEADS):
        low = h * 128 + (16 * h) % 128
        qtm[low : low + 16] = queries[16 * h : 16 * h + 16]

    def project(part, rows):
        keys[part * ROWS : (part + 1) * ROWS] = dot(rows, wqkv_ref[:, C : 2 * C]).astype(bf16)
        values = dot_nt(wv_t[...], rows).astype(bf16)
        vta[:, part * ROWS : (part + 1) * ROWS] = values

    project(0, normed)

    even, odd = (s_0, s_1), (s_2, s_3)

    def queries_of(u):
        return pl.ds(pl.multiple_of(u // 8 * QUERIES, QUERIES), QUERIES)

    def scores(bufs, u, low, count):
        highest = []
        for k, buf in enumerate(bufs):
            h = u % 8 * 2 + k
            q = qtm[pl.ds(pl.multiple_of(h * 128, 128), 128), queries_of(u)]
            s = dot(keys[low : low + count, pl.ds(pl.multiple_of(h // 8 * 128, 128), 128)], q)
            buf[:count] = s
            highest.append(jnp.max(s, axis=0, keepdims=True))
        return tuple(highest)

    def weigh(bufs, highest, u, low, count, keep):
        for k, buf in enumerate(bufs):
            h = u % 8 * 2 + k
            weights = jnp.exp2(buf[:count] - highest[k])
            total = jnp.sum(weights, axis=0, keepdims=True)
            v = vta[pl.ds(pl.multiple_of(h * WIDTH, WIDTH), WIDTH), low : low + count]
            keep(h, u, dot(v, weights.astype(bf16)), total, highest[k])

    def store(h, u, o, total, highest):
        att[pl.ds(pl.multiple_of(h * WIDTH, WIDTH), WIDTH), queries_of(u)] = (o * (1.0 / total)).astype(bf16)

    def store_part(h, u, o, total, highest):
        part_o[h] = o
        part_l[h] = jnp.broadcast_to(total, (8, QUERIES))
        part_m[h] = jnp.broadcast_to(highest, (8, QUERIES))

    def store_merged(h, u, o, total, highest):
        before = part_m[h][:1]
        top = jnp.maximum(before, highest)
        was, new = jnp.exp2(before - top), jnp.exp2(highest - top)
        store(h, u, part_o[h] * was + o * new, part_l[h][:1] * was + total * new, top)

    def two_units(u, highest, span, keep, then):
        second = scores(odd, u + 1, *span)
        weigh(even, highest, u, *span, keep)
        third = then()
        weigh(odd, second, u + 1, *span, keep)
        return third

    def sweep(first, count, highest, span, keep, ends=False):
        def step(i, highest):
            u = first + 2 * i
            return two_units(u, highest, span, keep, lambda: scores(even, u + 2, *span))

        highest = lax.fori_loop(0, count // 2 - (1 if ends else 0), step, highest)
        if ends:
            two_units(first + count - 2, highest, span, keep, lambda: None)
        return highest

    def back(block_ids, pages):
        for k in block_ids:
            p, m = place(OFFSETS[k])
            if pages is None:
                src, dst, at = out2.at[k], in2.at[me], 0
            else:
                src, dst, at = out2.at[k, pages], in2.at[me, pages], 1 + pages
            pltpu.make_async_remote_copy(
                src_ref=src, dst_ref=dst, send_sem=send2.at[at], recv_sem=recv2.at[at],
                device_id=(p, m), device_id_type=MESH,
            ).start()

    def back_half(half):
        rows = jnp.transpose(att[half * 128 : (half + 1) * 128])
        out2[FIRST:, half] = dot(comp_t[QUERIES:], rows).reshape(DEVS - FIRST, CAP, 128).astype(bf16)
        pltpu.make_async_copy(out2.at[DEVS - 1, half], in2.at[me, half], loc2.at[half]).start()
        back(range(FIRST, DEVS - 1), half)

    mine, other, whole = (0, ROWS), (ROWS, ROWS), (0, 2 * ROWS)
    sweep(0, 4, scores(even, 0, *mine), mine, store_part, ends=True)
    swap.wait()
    project(1, nrm[1])
    sweep(0, 4, scores(even, 0, *other), other, store_merged, ends=True)
    highest = sweep(4, 4, scores(even, 4, *whole), whole, store)
    rows = jnp.transpose(att[:, :QUERIES])
    slots = dot(comp_t[:QUERIES, :QUERIES], rows)
    for half in range(2):
        out2[:FIRST, half] = slots[:, half * 128 : (half + 1) * 128].reshape(FIRST, CAP, 128).astype(bf16)
    back(range(FIRST), None)
    highest = sweep(8, 4, highest, whole, store)
    back_half(0)
    sweep(12, 4, highest, whole, store, ends=True)
    back_half(1)

    def returned(half):
        pltpu.make_async_copy(out2.at[0, half], in2.at[0, half], loc2.at[half]).wait()
        came = in2.at[pl.ds(0, DEVS - 1 - FIRST), half]
        pltpu.make_async_copy(came, came, recv2.at[1 + half]).wait()
        return dot(bkt_t[...], in2[:, half].astype(f32).reshape(SLOTS, 128).astype(bf16)).astype(bf16)

    own_row = par_ref[...] - me * POOL
    member = onehot(iota((POOL, ROWS), 0) == own_row)
    ones = jnp.ones((ROWS, 128), bf16)
    counts = jnp.maximum(dot(member, ones), 1.0)
    edge_member = onehot(jnp.where(iota((16, ROWS), 0) < 8, -1, POOL - 1) == own_row)
    edge_counts = dot(edge_member, ones)
    own_cols = jnp.transpose(jnp.broadcast_to(own_row.astype(f32), (128, ROWS)))
    inner_t = jnp.concatenate(
        [onehot(jnp.where(own_cols == POOL - 1.0, -1.0, own_cols) == lanes + k * 128.0) for k in range(POOL // 128)],
        axis=1,
    )
    last_cols = jnp.where(own_cols == POOL - 1.0, 1.0, 0.0)
    spilled_cols = jnp.where(own_cols < 0.0, 1.0, 0.0)
    for k in range(2):
        e_out[k, :, C:] = edge_counts[8 * k : 8 * k + 8]

    came = in2.at[pl.ds(0, FIRST)]
    pltpu.make_async_copy(came, came, recv2.at[0]).wait()
    mixed = pt_ref[...].astype(f32)
    for half in range(2):
        mixed = mixed + dot(returned(half), wout_ref[half * 128 : (half + 1) * 128])
    encoded = mixed.astype(bf16)
    edge_sums = dot(edge_member, encoded)
    for k in range(2):
        e_out[k, :, :C] = edge_sums[8 * k : 8 * k + 8]

    def edge(k, line):
        return pltpu.make_async_remote_copy(
            src_ref=e_out.at[k], dst_ref=e_in.at[k], send_sem=esend.at[k], recv_sem=erecv.at[k],
            device_id=(line // 4, line % 4), device_id_type=MESH,
        )

    to_previous = edge(0, (me + DEVS - 1) % DEVS)
    to_next = edge(1, (me + 1) % DEVS)
    to_previous.start()
    to_next.start()

    def pool(sums, tallies):
        mean = sums / jnp.concatenate([tallies, tallies], axis=1)
        return gelu(layer_norm(dot(mean.astype(bf16), wpool_ref[...]))).astype(bf16)

    def lift(rows):
        return gelu(layer_norm(dot(rows, wup_ref[...]))).astype(bf16)

    pooled = pool(dot(member, encoded), counts)
    pooled_ref[...] = pooled
    skipped = gelu(layer_norm(dot(encoded, wskip_ref[...])))
    partial = skipped + dot(inner_t, lift(pooled))

    to_previous.wait()
    to_next.wait()
    shared = jnp.concatenate([e_out[1] + e_in[0], e_in[1] + e_out[0]], axis=0)
    shared_pooled = pool(shared[:, :C], jnp.maximum(shared[:, C:], 1.0))
    pooled_ref[POOL - 16 :] = jnp.where(iota((16, C2), 0) == 15, shared_pooled[:1], pooled[POOL - 16 :])
    shared_lifted = lift(shared_pooled).astype(f32)
    both = lambda v: jnp.concatenate([v, v], axis=1)
    picked = both(last_cols) * shared_lifted[:1] + both(spilled_cols) * shared_lifted[8:9]
    dec_ref[...] = (partial + picked).astype(bf16)

    most = out1.at[pl.ds(0, (DEVS - 1) * BLK)]
    pltpu.make_async_copy(most, most, send1).wait()
    most = out2.at[:FIRST]
    pltpu.make_async_copy(most, most, send2.at[0]).wait()
    for half in range(2):
        most = out2.at[FIRST : DEVS - 1, half]
        pltpu.make_async_copy(most, most, send2.at[1 + half]).wait()


def hand_out(pooled_ref, dec_ref, pooled_out, dec_out, sems):
    first = pltpu.make_async_copy(dec_ref, dec_out, sems.at[0])
    second = pltpu.make_async_copy(pooled_ref, pooled_out, sems.at[1])
    first.start()
    second.start()
    first.wait()
    second.wait()


def on_device(points, to_hilbert, parent, w_qkv, w_out, w_pool, w_up, w_skip):
    given = (points, to_hilbert.reshape(1, ROWS), parent.reshape(1, ROWS), w_qkv, w_out, w_pool, w_up, w_skip)
    vmem = pl.BlockSpec(memory_space=pltpu.VMEM)
    dma = pltpu.SemaphoreType.DMA
    held = [pltpu.with_memory_space_constraint(v, pltpu.HBM) for v in given]
    results = pl.pallas_call(
        kernel,
        out_shape=(pltpu.VMEM((POOL, C2), bf16), pltpu.VMEM((ROWS, C), bf16)),
        in_specs=[pl.BlockSpec(memory_space=pltpu.HBM)] * 8,
        out_specs=(vmem, vmem),
        scratch_shapes=[
            pltpu.VMEM((ROWS, C), bf16),
            pltpu.VMEM((1, ROWS), i32),
            pltpu.VMEM((1, ROWS), i32),
            pltpu.VMEM((C, 3 * C), bf16),
            pltpu.VMEM((C, C), bf16),
            pltpu.VMEM((C, C2), bf16),
            pltpu.VMEM((C2, C), bf16),
            pltpu.VMEM((C, C), bf16),
            pltpu.VMEM((DEVS * BLK, 128), bf16),
            pltpu.VMEM((DEVS * BLK, 128), bf16),
            pltpu.VMEM((DEVS, 2, CAP, 128), bf16),
            pltpu.VMEM((DEVS, 2, CAP, 128), bf16),
            pltpu.VMEM((ROWS, SLOTS), bf16),
            pltpu.VMEM((SLOTS, ROWS), bf16),
            pltpu.VMEM((C, C), bf16),
            pltpu.VMEM((C, C), bf16),
            pltpu.VMEM((2, ROWS, C), bf16),
            pltpu.VMEM((HEADS * 128, ROWS), bf16),
            pltpu.VMEM((C, 2 * ROWS), bf16),
            pltpu.VMEM((2 * ROWS, C), bf16),
            pltpu.VMEM((2 * ROWS, QUERIES), f32),
            pltpu.VMEM((2 * ROWS, QUERIES), f32),
            pltpu.VMEM((2 * ROWS, QUERIES), f32),
            pltpu.VMEM((2 * ROWS, QUERIES), f32),
            pltpu.VMEM((C, ROWS), bf16),
            pltpu.VMEM((HEADS // 2, WIDTH, QUERIES), f32),
            pltpu.VMEM((HEADS // 2, 8, QUERIES), f32),
            pltpu.VMEM((HEADS // 2, 8, QUERIES), f32),
            pltpu.VMEM((2, 8, C + 128), f32),
            pltpu.VMEM((2, 8, C + 128), f32),
            dma, dma, dma, dma((3,)), dma((3,)), dma((2,)), dma, dma, dma((2,)), dma((2,)), dma((8,)),
        ],
        compiler_params=pltpu.CompilerParams(
            collective_id=0, has_side_effects=True, vmem_limit_bytes=48 * 1024 * 1024
        ),
    )(*held)
    results = [pltpu.with_memory_space_constraint(v, pltpu.VMEM) for v in results]
    anywhere = pl.BlockSpec(memory_space=pl.ANY)
    return pl.pallas_call(
        hand_out,
        out_shape=(jax.ShapeDtypeStruct((POOL, C2), bf16), jax.ShapeDtypeStruct((ROWS, C), bf16)),
        in_specs=[vmem, vmem],
        out_specs=(anywhere, anywhere),
        scratch_shapes=[dma((2,))],
    )(*results)


def solution(mesh):
    rows = P(("pts", "mdl"), None)
    flat = P(("pts", "mdl"))
    return jax.shard_map(
        on_device,
        mesh=mesh,
        in_specs=(rows, flat, flat, P(), P(), P(), P(), P()),
        out_specs=(rows, rows),
        check_vma=False,
    )
```

```python
import functools

import jax
import jax.numpy as jnp
from jax import lax
from jax.experimental import pallas as pl
from jax.experimental.pallas import tpu as pltpu
from jax.sharding import PartitionSpec as P

ROWS = 512
C = 256
C2 = 512
HEADS = 16
WIDTH = C // HEADS
POOL = ROWS // 2
DEVS = 128
CAP = 8
SLOTS = DEVS * CAP
BLK = 2 * CAP
EMPTY = 64.0
QSCALE = WIDTH**-0.5 * 1.4426950408889634
MESH = pl.DeviceIdType.MESH
f32, bf16, i32 = jnp.float32, jnp.bfloat16, jnp.int32


def _offsets():
    far = lambda d: min(d, 4 - d)
    every = [(x, y, c, z) for x in range(4) for y in range(4) for z in range(4) for c in range(2)]
    every.sort(key=lambda o: -(far(o[0]) + far(o[1]) + far(o[3]) + 0.1 * o[2]))
    return [o for o in every if any(o)]


OFFSETS = _offsets()
FIRST = 32
QUERIES = FIRST * CAP


def minus(o):
    return tuple((-v) % (2 if k == 2 else 4) for k, v in enumerate(o))


def dot(a, b):
    return jnp.dot(a, b, preferred_element_type=f32)


def dot_nt(a, b):
    return lax.dot_general(a, b, (((1,), (1,)), ((), ())), preferred_element_type=f32)


def dot_tn(a, b):
    return lax.dot_general(a, b, (((0,), (0,)), ((), ())), preferred_element_type=f32)


def iota(shape, dim):
    return lax.broadcasted_iota(i32, shape, dim)


def onehot(cond):
    return jnp.where(cond, 1.0, 0.0).astype(bf16)


def layer_norm(v):
    center = v - jnp.mean(v, axis=-1, keepdims=True)
    spread = jnp.mean(center * center, axis=-1, keepdims=True)
    return center * lax.rsqrt(spread + 1e-5)


def gelu(v):
    return 0.5 * v * (1.0 + jnp.tanh(0.7978845608028654 * (v + 0.044715 * (v * v * v))))


def to_blocks(v):
    v = v.reshape(DEVS, CAP, C)
    return jnp.concatenate([v[:, :, :128], v[:, :, 128:]], axis=1).reshape(DEVS * BLK, 128)


def kernel(
    *refs,
):
    (given, (pooled_ref, dec_ref), held, rest) = refs[:8], refs[8:10], refs[10:18], refs[18:]
    pt_ref, th_ref, par_ref, wqkv_ref, wout_ref, wpool_ref, wup_ref, wskip_ref = held
    (
    out1, in1, out2, in2, bkt_t, comp_t, wq_t, wv_t, nrm, qtm, vta, keys, s_0, s_1, s_2, s_3, att, part_o, part_l, part_m, e_out, e_in,
    send1, recv1, loc1, send2, recv2, loc2, psend, precv, esend, erecv, fetched,
    ) = rest
    loads = [pltpu.make_async_copy(given[i], held[i], fetched.at[i]) for i in range(8)]
    pts, mdl = lax.axis_index("pts"), lax.axis_index("mdl")
    me = pts * 4 + mdl
    core, yy, xx = pts % 2, (pts // 2) % 4, pts // 8
    at_x = [((xx + d) % 4) * 8 for d in range(4)]
    at_y = [((yy + d) % 4) * 2 for d in range(4)]
    at_c = [(core + d) % 2 for d in range(2)]
    at_z = [(mdl + d) % 4 for d in range(4)]

    def place(o):
        return at_x[o[0]] + at_y[o[1]] + at_c[o[2]], at_z[o[3]]

    def block(line):
        return pl.ds(pl.multiple_of(line * BLK, BLK), BLK)

    barrier = pltpu.get_barrier_semaphore()
    for k, o in enumerate(OFFSETS):
        pl.semaphore_signal(barrier, inc=1, device_id=place(o), device_id_type=MESH)
        if k == 15:
            for i in (1, 0, 2, 3, 4, 7, 5, 6):
                loads[i].start()

    loads[1].wait()
    half = th_ref[...] >> 9
    target = (half >> 3) * 8 + (half & 1) * 4 + ((half >> 1) & 3)
    match = jnp.where(iota((DEVS, ROWS), 0) == target, 1.0, 0.0)
    upper = onehot(iota((ROWS, ROWS), 0) < iota((ROWS, ROWS), 1))
    earlier = dot(match.astype(bf16), upper)
    rank = jnp.sum(match * earlier, axis=0, keepdims=True)
    slot = target * CAP + rank.astype(i32)
    bucket = jnp.where(iota((SLOTS, ROWS), 0) == slot, 1.0, 0.0)
    taken = jnp.sum(bucket, axis=1, keepdims=True)
    loads[0].wait()
    normed = layer_norm(pt_ref[...].astype(f32)).astype(bf16)
    filled = dot(bucket.astype(bf16), normed)
    lane = iota((1, C), 1)
    filled = filled + jnp.where(lane < 128, (1.0 - taken) * EMPTY, 0.0)
    out1[...] = to_blocks(filled).astype(bf16)

    pl.semaphore_wait(barrier, DEVS - 1)

    last = (DEVS - 1) * BLK
    own = pltpu.make_async_copy(out1.at[block(me)], in1.at[pl.ds(last, BLK)], loc1)
    own.start()
    for o in OFFSETS:
        p, m = place(o)
        pltpu.make_async_remote_copy(
            src_ref=out1.at[block(p * 4 + m)],
            dst_ref=in1.at[pl.ds(OFFSETS.index(minus(o)) * BLK, BLK)],
            send_sem=send1,
            recv_sem=recv1,
            device_id=(p, m),
            device_id_type=MESH,
        ).start()

    slot_cols = jnp.transpose(jnp.broadcast_to(slot.astype(f32), (128, ROWS)))
    lanes = iota((1, 128), 1).astype(f32)
    for k in range(SLOTS // 128):
        bkt_t[:, k * 128 : (k + 1) * 128] = onehot(slot_cols == lanes + k * 128.0)
    for i in range(2, 8):
        loads[i].wait()
    wq_t[...] = jnp.transpose(wqkv_ref[:, :C])
    wv_t[...] = jnp.transpose(wqkv_ref[:, 2 * C :])
    qtm[...] = jnp.zeros_like(qtm)
    sublane = iota((DEVS, CAP, 128), 1).astype(f32)
    pick = jnp.where(iota((16, 128), 1) == 0, 32.0, jnp.where(iota((16, 128), 1) == 64, 1.0, 0.0)).astype(bf16)

    own.wait()
    came = in1.at[pl.ds(0, last)]
    pltpu.make_async_copy(came, came, recv1).wait()
    halves = in1[...].astype(f32).reshape(DEVS, BLK, 128)
    valid = jnp.where(halves[:, :CAP] < 32.0, 1.0, 0.0)
    counts = jnp.sum(valid, axis=1, keepdims=True)
    upto = counts
    for step in (1, 2, 4, 8, 16, 32, 64):
        upto = upto + jnp.concatenate([jnp.zeros((step, 1, 128), f32), upto[:-step]], axis=0)
    place_of = jnp.where(valid > 0.0, upto - counts + sublane, -1.0).reshape(SLOTS, 128)
    high = jnp.floor(place_of * (1.0 / 32.0))
    digits = jnp.where(iota((SLOTS, 128), 1) < 64, high, place_of - 32.0 * high).astype(bf16)
    place_row = dot_nt(pick, digits)[:1].astype(i32)
    comp = onehot(iota((ROWS, SLOTS), 0) == place_row)
    arrived = jnp.concatenate([halves[:, :CAP], halves[:, CAP:]], axis=2).reshape(SLOTS, C).astype(bf16)
    normed = dot(comp, arrived).astype(bf16)
    nrm[0] = normed

    swap = pltpu.make_async_remote_copy(
        src_ref=nrm.at[0], dst_ref=nrm.at[1], send_sem=psend, recv_sem=precv,
        device_id=(at_x[0] + at_y[0] + at_c[1], mdl), device_id_type=MESH,
    )
    swap.start()

    for c in range(ROWS // 128):
        comp_t[:, c * 128 : (c + 1) * 128] = onehot(place_of == lanes + c * 128.0)
    queries = (dot_nt(wq_t[...], normed) * QSCALE).astype(bf16)
    for h in range(HEADS):
        low = h * 128 + (16 * h) % 128
        qtm[low : low + 16] = queries[16 * h : 16 * h + 16]

    def project(part, rows):
        keys[part * ROWS : (part + 1) * ROWS] = dot(rows, wqkv_ref[:, C : 2 * C]).astype(bf16)
        values = dot_nt(wv_t[...], rows).astype(bf16)
        vta[:, part * ROWS : (part + 1) * ROWS] = values

    project(0, normed)

    even, odd = (s_0, s_1), (s_2, s_3)

    def queries_of(u):
        return pl.ds(pl.multiple_of(u // 8 * QUERIES, QUERIES), QUERIES)

    def scores(bufs, u, low, count):
        highest = []
        for k, buf in enumerate(bufs):
            h = u % 8 * 2 + k
            q = qtm[pl.ds(pl.multiple_of(h * 128, 128), 128), queries_of(u)]
            s = dot(keys[low : low + count, pl.ds(pl.multiple_of(h // 8 * 128, 128), 128)], q)
            buf[:count] = s
            highest.append(jnp.max(s, axis=0, keepdims=True))
        return tuple(highest)

    def weigh(bufs, highest, u, low, count, keep):
        for k, buf in enumerate(bufs):
            h = u % 8 * 2 + k
            weights = jnp.exp2(buf[:count] - highest[k])
            total = jnp.sum(weights, axis=0, keepdims=True)
            v = vta[pl.ds(pl.multiple_of(h * WIDTH, WIDTH), WIDTH), low : low + count]
            keep(h, u, dot(v, weights.astype(bf16)), total, highest[k])

    def store(h, u, o, total, highest):
        att[pl.ds(pl.multiple_of(h * WIDTH, WIDTH), WIDTH), queries_of(u)] = (o * (1.0 / total)).astype(bf16)

    def store_part(h, u, o, total, highest):
        part_o[h] = o
        part_l[h] = jnp.broadcast_to(total, (8, QUERIES))
        part_m[h] = jnp.broadcast_to(highest, (8, QUERIES))

    def store_merged(h, u, o, total, highest):
        before = part_m[h][:1]
        top = jnp.maximum(before, highest)
        was, new = jnp.exp2(before - top), jnp.exp2(highest - top)
        store(h, u, part_o[h] * was + o * new, part_l[h][:1] * was + total * new, top)

    def two_units(u, highest, span, keep, then):
        second = scores(odd, u + 1, *span)
        weigh(even, highest, u, *span, keep)
        third = then()
        weigh(odd, second, u + 1, *span, keep)
        return third

    def sweep(first, count, highest, span, keep, ends=False):
        def step(i, highest):
            u = first + 2 * i
            return two_units(u, highest, span, keep, lambda: scores(even, u + 2, *span))

        highest = lax.fori_loop(0, count // 2 - (1 if ends else 0), step, highest)
        if ends:
            two_units(first + count - 2, highest, span, keep, lambda: None)
        return highest

    def back(block_ids, pages):
        for k in block_ids:
            p, m = place(OFFSETS[k])
            if pages is None:
                src, dst, at = out2.at[k], in2.at[me], 0
            else:
                src, dst, at = out2.at[k, pages], in2.at[me, pages], 1 + pages
            pltpu.make_async_remote_copy(
                src_ref=src, dst_ref=dst, send_sem=send2.at[at], recv_sem=recv2.at[at],
                device_id=(p, m), device_id_type=MESH,
            ).start()

    def back_half(half):
        slots = dot_nt(comp_t[QUERIES:], att[half * 128 : (half + 1) * 128])
        out2[FIRST:, half] = slots.reshape(DEVS - FIRST, CAP, 128).astype(bf16)
        pltpu.make_async_copy(out2.at[DEVS - 1, half], in2.at[me, half], loc2.at[half]).start()
        back(range(FIRST, DEVS - 1), half)

    mine, other, whole = (0, ROWS), (ROWS, ROWS), (0, 2 * ROWS)
    sweep(0, 4, scores(even, 0, *mine), mine, store_part, ends=True)
    swap.wait()
    project(1, nrm[1])
    sweep(0, 4, scores(even, 0, *other), other, store_merged, ends=True)
    highest = sweep(4, 4, scores(even, 4, *whole), whole, store)
    slots = dot_nt(comp_t[:QUERIES, :QUERIES], att[:, :QUERIES])
    for half in range(2):
        out2[:FIRST, half] = slots[:, half * 128 : (half + 1) * 128].reshape(FIRST, CAP, 128).astype(bf16)
    back(range(FIRST), None)
    highest = sweep(8, 4, highest, whole, store)
    back_half(0)
    sweep(12, 4, highest, whole, store, ends=True)
    back_half(1)

    def returned(half):
        pltpu.make_async_copy(out2.at[0, half], in2.at[0, half], loc2.at[half]).wait()
        came = in2.at[pl.ds(0, DEVS - 1 - FIRST), half]
        pltpu.make_async_copy(came, came, recv2.at[1 + half]).wait()
        return in2[:, half].astype(f32).reshape(SLOTS, 128).astype(bf16)

    own_row = par_ref[...] - me * POOL
    member = onehot(iota((POOL, ROWS), 0) == own_row)
    ones = jnp.ones((ROWS, 128), bf16)
    counts = jnp.maximum(dot(member, ones), 1.0)
    edge_member = onehot(jnp.where(iota((16, ROWS), 0) < 8, -1, POOL - 1) == own_row)
    edge_counts = dot(edge_member, ones)
    edge_slots = dot(edge_member, bkt_t[...]).astype(bf16)
    edge_sums = dot(edge_member, pt_ref[...])
    own_cols = jnp.transpose(jnp.broadcast_to(own_row.astype(f32), (128, ROWS)))
    inner_t = jnp.concatenate(
        [onehot(jnp.where(own_cols == POOL - 1.0, -1.0, own_cols) == lanes + k * 128.0) for k in range(POOL // 128)],
        axis=1,
    )
    last_cols = jnp.where(own_cols == POOL - 1.0, 1.0, 0.0)
    spilled_cols = jnp.where(own_cols < 0.0, 1.0, 0.0)
    for k in range(2):
        e_out[k, :, C:] = edge_counts[8 * k : 8 * k + 8]

    came = in2.at[pl.ds(0, FIRST)]
    pltpu.make_async_copy(came, came, recv2.at[0]).wait()
    slots = []
    for half in range(2):
        slots.append(returned(half))
        sums = dot(edge_slots, slots[half])
        high = sums.astype(bf16)
        both_parts = jnp.concatenate([high, (sums - high.astype(f32)).astype(bf16)], axis=0)
        parts = dot(both_parts, wout_ref[half * 128 : (half + 1) * 128])
        edge_sums = edge_sums + parts[:16] + parts[16:]
    for k in range(2):
        e_out[k, :, :C] = edge_sums[8 * k : 8 * k + 8]

    def edge(k, line):
        return pltpu.make_async_remote_copy(
            src_ref=e_out.at[k], dst_ref=e_in.at[k], send_sem=esend.at[k], recv_sem=erecv.at[k],
            device_id=(line // 4, line % 4), device_id_type=MESH,
        )

    to_previous = edge(0, (me + DEVS - 1) % DEVS)
    to_next = edge(1, (me + 1) % DEVS)

    @pl.when(me > 0)
    def _():
        to_previous.start()

    @pl.when(me == 0)
    def _():
        e_in[1] = jnp.zeros((8, C + 128), f32)

    @pl.when(me < DEVS - 1)
    def _():
        to_next.start()

    @pl.when(me == DEVS - 1)
    def _():
        e_in[0] = jnp.zeros((8, C + 128), f32)

    mixed = pt_ref[...].astype(f32)
    for half in range(2):
        attended = dot(bkt_t[...], slots[half]).astype(bf16)
        mixed = mixed + dot(attended, wout_ref[half * 128 : (half + 1) * 128])
    encoded = mixed.astype(bf16)

    def pool(sums, tallies):
        mean = sums / jnp.concatenate([tallies, tallies], axis=1)
        return gelu(layer_norm(dot(mean.astype(bf16), wpool_ref[...]))).astype(bf16)

    def lift(rows):
        return gelu(layer_norm(dot(rows, wup_ref[...]))).astype(bf16)

    pooled = pool(dot(member, encoded), counts)
    pooled_ref[...] = pooled
    skipped = gelu(layer_norm(dot(encoded, wskip_ref[...])))
    partial = skipped + dot(inner_t, lift(pooled))

    @pl.when(me > 0)
    def _():
        to_previous.wait_send()
        to_next.wait_recv()

    @pl.when(me < DEVS - 1)
    def _():
        to_next.wait_send()
        to_previous.wait_recv()

    shared = jnp.concatenate([e_out[1] + e_in[0], e_in[1] + e_out[0]], axis=0)
    shared_pooled = pool(shared[:, :C], jnp.maximum(shared[:, C:], 1.0))
    pooled_ref[POOL - 16 :] = jnp.where(iota((16, C2), 0) == 15, shared_pooled[:1], pooled[POOL - 16 :])
    shared_lifted = lift(shared_pooled).astype(f32)
    both = lambda v: jnp.concatenate([v, v], axis=1)
    picked = both(last_cols) * shared_lifted[:1] + both(spilled_cols) * shared_lifted[8:9]
    dec_ref[...] = (partial + picked).astype(bf16)

    most = out1.at[pl.ds(0, (DEVS - 1) * BLK)]
    pltpu.make_async_copy(most, most, send1).wait()
    most = out2.at[:FIRST]
    pltpu.make_async_copy(most, most, send2.at[0]).wait()
    for half in range(2):
        most = out2.at[FIRST : DEVS - 1, half]
        pltpu.make_async_copy(most, most, send2.at[1 + half]).wait()


def hand_out(pooled_ref, dec_ref, pooled_out, dec_out, sems):
    first = pltpu.make_async_copy(dec_ref, dec_out, sems.at[0])
    second = pltpu.make_async_copy(pooled_ref, pooled_out, sems.at[1])
    first.start()
    second.start()
    first.wait()
    second.wait()


def on_device(points, to_hilbert, parent, w_qkv, w_out, w_pool, w_up, w_skip):
    given = (points, to_hilbert.reshape(1, ROWS), parent.reshape(1, ROWS), w_qkv, w_out, w_pool, w_up, w_skip)
    vmem = pl.BlockSpec(memory_space=pltpu.VMEM)
    dma = pltpu.SemaphoreType.DMA
    held = [pltpu.with_memory_space_constraint(v, pltpu.HBM) for v in given]
    results = pl.pallas_call(
        kernel,
        out_shape=(pltpu.VMEM((POOL, C2), bf16), pltpu.VMEM((ROWS, C), bf16)),
        in_specs=[pl.BlockSpec(memory_space=pltpu.HBM)] * 8,
        out_specs=(vmem, vmem),
        scratch_shapes=[
            pltpu.VMEM((ROWS, C), bf16),
            pltpu.VMEM((1, ROWS), i32),
            pltpu.VMEM((1, ROWS), i32),
            pltpu.VMEM((C, 3 * C), bf16),
            pltpu.VMEM((C, C), bf16),
            pltpu.VMEM((C, C2), bf16),
            pltpu.VMEM((C2, C), bf16),
            pltpu.VMEM((C, C), bf16),
            pltpu.VMEM((DEVS * BLK, 128), bf16),
            pltpu.VMEM((DEVS * BLK, 128), bf16),
            pltpu.VMEM((DEVS, 2, CAP, 128), bf16),
            pltpu.VMEM((DEVS, 2, CAP, 128), bf16),
            pltpu.VMEM((ROWS, SLOTS), bf16),
            pltpu.VMEM((SLOTS, ROWS), bf16),
            pltpu.VMEM((C, C), bf16),
            pltpu.VMEM((C, C), bf16),
            pltpu.VMEM((2, ROWS, C), bf16),
            pltpu.VMEM((HEADS * 128, ROWS), bf16),
            pltpu.VMEM((C, 2 * ROWS), bf16),
            pltpu.VMEM((2 * ROWS, C), bf16),
            pltpu.VMEM((2 * ROWS, QUERIES), f32),
            pltpu.VMEM((2 * ROWS, QUERIES), f32),
            pltpu.VMEM((2 * ROWS, QUERIES), f32),
            pltpu.VMEM((2 * ROWS, QUERIES), f32),
            pltpu.VMEM((C, ROWS), bf16),
            pltpu.VMEM((HEADS // 2, WIDTH, QUERIES), f32),
            pltpu.VMEM((HEADS // 2, 8, QUERIES), f32),
            pltpu.VMEM((HEADS // 2, 8, QUERIES), f32),
            pltpu.VMEM((2, 8, C + 128), f32),
            pltpu.VMEM((2, 8, C + 128), f32),
            dma, dma, dma, dma((3,)), dma((3,)), dma((2,)), dma, dma, dma((2,)), dma((2,)), dma((8,)),
        ],
        compiler_params=pltpu.CompilerParams(
            collective_id=0, has_side_effects=True, vmem_limit_bytes=48 * 1024 * 1024
        ),
    )(*held)
    results = [pltpu.with_memory_space_constraint(v, pltpu.VMEM) for v in results]
    anywhere = pl.BlockSpec(memory_space=pl.ANY)
    return pl.pallas_call(
        hand_out,
        out_shape=(jax.ShapeDtypeStruct((POOL, C2), bf16), jax.ShapeDtypeStruct((ROWS, C), bf16)),
        in_specs=[vmem, vmem],
        out_specs=(anywhere, anywhere),
        scratch_shapes=[dma((2,))],
    )(*results)


def solution(mesh):
    rows = P(("pts", "mdl"), None)
    flat = P(("pts", "mdl"))
    return jax.shard_map(
        on_device,
        mesh=mesh,
        in_specs=(rows, flat, flat, P(), P(), P(), P(), P()),
        out_specs=(rows, rows),
        check_vma=False,
    )
```

```python
import functools

import jax
import jax.numpy as jnp
from jax import lax
from jax.experimental import pallas as pl
from jax.experimental.pallas import tpu as pltpu
from jax.sharding import PartitionSpec as P

ROWS = 512
C = 256
C2 = 512
HEADS = 16
WIDTH = C // HEADS
POOL = ROWS // 2
DEVS = 128
CAP = 8
SLOTS = DEVS * CAP
BLK = 2 * CAP
EMPTY = 64.0
QSCALE = WIDTH**-0.5 * 1.4426950408889634
MESH = pl.DeviceIdType.MESH
f32, bf16, i32 = jnp.float32, jnp.bfloat16, jnp.int32


def _offsets():
    far = lambda d: min(d, 4 - d)
    every = [(x, y, c, z) for x in range(4) for y in range(4) for z in range(4) for c in range(2)]
    mixed = lambda o: (o[0] * 7 + o[1] * 5 + o[3] * 3 + o[2] * 11) % 13
    every.sort(key=lambda o: -(far(o[0]) + far(o[1]) + far(o[3]) + 0.01 * mixed(o)))
    return [o for o in every if any(o)]


OFFSETS = _offsets()
FIRST = 32
QUERIES = FIRST * CAP


def minus(o):
    return tuple((-v) % (2 if k == 2 else 4) for k, v in enumerate(o))


def dot(a, b):
    return jnp.dot(a, b, preferred_element_type=f32)


def dot_nt(a, b):
    return lax.dot_general(a, b, (((1,), (1,)), ((), ())), preferred_element_type=f32)


def dot_tn(a, b):
    return lax.dot_general(a, b, (((0,), (0,)), ((), ())), preferred_element_type=f32)


def iota(shape, dim):
    return lax.broadcasted_iota(i32, shape, dim)


def onehot(cond):
    return jnp.where(cond, 1.0, 0.0).astype(bf16)


def layer_norm(v):
    center = v - jnp.mean(v, axis=-1, keepdims=True)
    spread = jnp.mean(center * center, axis=-1, keepdims=True)
    return center * lax.rsqrt(spread + 1e-5)


def gelu(v):
    return 0.5 * v * (1.0 + jnp.tanh(0.7978845608028654 * (v + 0.044715 * (v * v * v))))


def to_blocks(v):
    v = v.reshape(DEVS, CAP, C)
    return jnp.concatenate([v[:, :, :128], v[:, :, 128:]], axis=1).reshape(DEVS * BLK, 128)


def kernel(
    *refs,
):
    (given, (pooled_ref, dec_ref), held, rest) = refs[:8], refs[8:10], refs[10:18], refs[18:]
    pt_ref, th_ref, par_ref, wqkv_ref, wout_ref, wpool_ref, wup_ref, wskip_ref = held
    (
    out1, in1, out2, in2, bkt_t, comp_t, wq_t, wv_t, nrm, qtm, vta, keys, s_0, s_1, s_2, s_3, att, part_o, part_l, part_m, e_out, e_in,
    send1, recv1, loc1, send2, recv2, loc2, psend, precv, esend, erecv, fetched,
    ) = rest
    loads = [pltpu.make_async_copy(given[i], held[i], fetched.at[i]) for i in range(8)]
    pts, mdl = lax.axis_index("pts"), lax.axis_index("mdl")
    me = pts * 4 + mdl
    core, yy, xx = pts % 2, (pts // 2) % 4, pts // 8
    at_x = [((xx + d) % 4) * 8 for d in range(4)]
    at_y = [((yy + d) % 4) * 2 for d in range(4)]
    at_c = [(core + d) % 2 for d in range(2)]
    at_z = [(mdl + d) % 4 for d in range(4)]

    def place(o):
        return at_x[o[0]] + at_y[o[1]] + at_c[o[2]], at_z[o[3]]

    def block(line):
        return pl.ds(pl.multiple_of(line * BLK, BLK), BLK)

    barrier = pltpu.get_barrier_semaphore()
    for k, o in enumerate(OFFSETS):
        pl.semaphore_signal(barrier, inc=1, device_id=place(o), device_id_type=MESH)
        if k == 15:
            for i in (1, 0, 2, 3, 4, 7, 5, 6):
                loads[i].start()

    loads[1].wait()
    half = th_ref[...] >> 9
    target = (half >> 3) * 8 + (half & 1) * 4 + ((half >> 1) & 3)
    match = jnp.where(iota((DEVS, ROWS), 0) == target, 1.0, 0.0)
    upper = onehot(iota((ROWS, ROWS), 0) < iota((ROWS, ROWS), 1))
    earlier = dot(match.astype(bf16), upper)
    rank = jnp.sum(match * earlier, axis=0, keepdims=True)
    slot = target * CAP + rank.astype(i32)
    bucket = jnp.where(iota((SLOTS, ROWS), 0) == slot, 1.0, 0.0)
    taken = jnp.sum(bucket, axis=1, keepdims=True)
    loads[0].wait()
    normed = layer_norm(pt_ref[...].astype(f32)).astype(bf16)
    filled = dot(bucket.astype(bf16), normed)
    lane = iota((1, C), 1)
    filled = filled + jnp.where(lane < 128, (1.0 - taken) * EMPTY, 0.0)
    out1[...] = to_blocks(filled).astype(bf16)

    pl.semaphore_wait(barrier, DEVS - 1)

    last = (DEVS - 1) * BLK
    own = pltpu.make_async_copy(out1.at[block(me)], in1.at[pl.ds(last, BLK)], loc1)
    own.start()
    for o in OFFSETS:
        p, m = place(o)
        pltpu.make_async_remote_copy(
            src_ref=out1.at[block(p * 4 + m)],
            dst_ref=in1.at[pl.ds(OFFSETS.index(minus(o)) * BLK, BLK)],
            send_sem=send1,
            recv_sem=recv1,
            device_id=(p, m),
            device_id_type=MESH,
        ).start()

    slot_cols = jnp.transpose(jnp.broadcast_to(slot.astype(f32), (128, ROWS)))
    lanes = iota((1, 128), 1).astype(f32)
    for k in range(SLOTS // 128):
        bkt_t[:, k * 128 : (k + 1) * 128] = onehot(slot_cols == lanes + k * 128.0)
    for i in range(2, 8):
        loads[i].wait()
    wq_t[...] = jnp.transpose(wqkv_ref[:, :C])
    wv_t[...] = jnp.transpose(wqkv_ref[:, 2 * C :])
    qtm[...] = jnp.zeros_like(qtm)
    sublane = iota((DEVS, CAP, 128), 1).astype(f32)
    pick = jnp.where(iota((16, 128), 1) == 0, 32.0, jnp.where(iota((16, 128), 1) == 64, 1.0, 0.0)).astype(bf16)

    own.wait()
    came = in1.at[pl.ds(0, last)]
    pltpu.make_async_copy(came, came, recv1).wait()
    halves = in1[...].astype(f32).reshape(DEVS, BLK, 128)
    valid = jnp.where(halves[:, :CAP] < 32.0, 1.0, 0.0)
    counts = jnp.sum(valid, axis=1, keepdims=True)
    upto = counts
    for step in (1, 2, 4, 8, 16, 32, 64):
        upto = upto + jnp.concatenate([jnp.zeros((step, 1, 128), f32), upto[:-step]], axis=0)
    place_of = jnp.where(valid > 0.0, upto - counts + sublane, -1.0).reshape(SLOTS, 128)
    high = jnp.floor(place_of * (1.0 / 32.0))
    digits = jnp.where(iota((SLOTS, 128), 1) < 64, high, place_of - 32.0 * high).astype(bf16)
    place_row = dot_nt(pick, digits)[:1].astype(i32)
    comp = onehot(iota((ROWS, SLOTS), 0) == place_row)
    arrived = jnp.concatenate([halves[:, :CAP], halves[:, CAP:]], axis=2).reshape(SLOTS, C).astype(bf16)
    normed = dot(comp, arrived).astype(bf16)
    nrm[0] = normed

    swap = pltpu.make_async_remote_copy(
        src_ref=nrm.at[0], dst_ref=nrm.at[1], send_sem=psend, recv_sem=precv,
        device_id=(at_x[0] + at_y[0] + at_c[1], mdl), device_id_type=MESH,
    )
    swap.start()

    for c in range(ROWS // 128):
        comp_t[:, c * 128 : (c + 1) * 128] = onehot(place_of == lanes + c * 128.0)
    queries = (dot_nt(wq_t[...], normed) * QSCALE).astype(bf16)
    for h in range(HEADS):
        low = h * 128 + (16 * h) % 128
        qtm[low : low + 16] = queries[16 * h : 16 * h + 16]

    def project(part, rows):
        keys[part * ROWS : (part + 1) * ROWS] = dot(rows, wqkv_ref[:, C : 2 * C]).astype(bf16)
        values = dot_nt(wv_t[...], rows).astype(bf16)
        vta[:, part * ROWS : (part + 1) * ROWS] = values

    project(0, normed)

    even, odd = (s_0, s_1), (s_2, s_3)

    def queries_of(u):
        return pl.ds(pl.multiple_of(u // 8 * QUERIES, QUERIES), QUERIES)

    def scores(bufs, u, low, count):
        highest = []
        for k, buf in enumerate(bufs):
            h = u % 8 * 2 + k
            q = qtm[pl.ds(pl.multiple_of(h * 128, 128), 128), queries_of(u)]
            s = dot(keys[low : low + count, pl.ds(pl.multiple_of(h // 8 * 128, 128), 128)], q)
            buf[:count] = s
            highest.append(jnp.max(s, axis=0, keepdims=True))
        return tuple(highest)

    def weigh(bufs, highest, u, low, count, keep):
        for k, buf in enumerate(bufs):
            h = u % 8 * 2 + k
            weights = jnp.exp2(buf[:count] - highest[k])
            total = jnp.sum(weights, axis=0, keepdims=True)
            v = vta[pl.ds(pl.multiple_of(h * WIDTH, WIDTH), WIDTH), low : low + count]
            keep(h, u, dot(v, weights.astype(bf16)), total, highest[k])

    def store(h, u, o, total, highest):
        att[pl.ds(pl.multiple_of(h * WIDTH, WIDTH), WIDTH), queries_of(u)] = (o * (1.0 / total)).astype(bf16)

    def store_part(h, u, o, total, highest):
        part_o[h] = o
        part_l[h] = jnp.broadcast_to(total, (8, QUERIES))
        part_m[h] = jnp.broadcast_to(highest, (8, QUERIES))

    def store_merged(h, u, o, total, highest):
        before = part_m[h][:1]
        top = jnp.maximum(before, highest)
        was, new = jnp.exp2(before - top), jnp.exp2(highest - top)
        store(h, u, part_o[h] * was + o * new, part_l[h][:1] * was + total * new, top)

    def two_units(u, highest, span, keep, then):
        second = scores(odd, u + 1, *span)
        weigh(even, highest, u, *span, keep)
        third = then()
        weigh(odd, second, u + 1, *span, keep)
        return third

    def sweep(first, count, highest, span, keep, then=None):
        def step(i, highest):
            u = first + 2 * i
            return two_units(u, highest, span, keep, lambda: scores(even, u + 2, *span))

        if then is None:
            return lax.fori_loop(0, count // 2, step, highest)
        highest = lax.fori_loop(0, count // 2 - 1, step, highest)
        return two_units(first + count - 2, highest, span, keep, then)

    def back(block_ids, pages):
        for k in block_ids:
            p, m = place(OFFSETS[k])
            if pages is None:
                src, dst, at = out2.at[k], in2.at[me], 0
            else:
                src, dst, at = out2.at[k, pages], in2.at[me, pages], 1 + pages
            pltpu.make_async_remote_copy(
                src_ref=src, dst_ref=dst, send_sem=send2.at[at], recv_sem=recv2.at[at],
                device_id=(p, m), device_id_type=MESH,
            ).start()

    def back_half(half):
        slots = dot_nt(comp_t[QUERIES:], att[half * 128 : (half + 1) * 128])
        out2[FIRST:, half] = slots.reshape(DEVS - FIRST, CAP, 128).astype(bf16)
        pltpu.make_async_copy(out2.at[DEVS - 1, half], in2.at[me, half], loc2.at[half]).start()
        back(range(FIRST, DEVS - 1), half)

    mine, other, whole = (0, ROWS), (ROWS, ROWS), (0, 2 * ROWS)
    def partner():
        swap.wait()
        project(1, nrm[1])
        return scores(even, 0, *other)

    sweep(0, 4, scores(even, 0, *mine), mine, store_part, lambda: None)
    highest = partner()
    highest = sweep(0, 4, highest, other, store_merged, lambda: scores(even, 4, *whole))
    highest = sweep(4, 4, highest, whole, store)
    slots = dot_nt(comp_t[:QUERIES, :QUERIES], att[:, :QUERIES])
    for half in range(2):
        out2[:FIRST, half] = slots[:, half * 128 : (half + 1) * 128].reshape(FIRST, CAP, 128).astype(bf16)
    back(range(FIRST), None)
    highest = sweep(8, 4, highest, whole, store)
    back_half(0)
    sweep(12, 4, highest, whole, store, lambda: None)
    back_half(1)

    def returned(half):
        pltpu.make_async_copy(out2.at[0, half], in2.at[0, half], loc2.at[half]).wait()
        came = in2.at[pl.ds(0, DEVS - 1 - FIRST), half]
        pltpu.make_async_copy(came, came, recv2.at[1 + half]).wait()
        return in2[:, half].astype(f32).reshape(SLOTS, 128).astype(bf16)

    own_row = par_ref[...] - me * POOL
    member = onehot(iota((POOL, ROWS), 0) == own_row)
    ones = jnp.ones((ROWS, 128), bf16)
    counts = jnp.maximum(dot(member, ones), 1.0)
    edge_member = onehot(jnp.where(iota((16, ROWS), 0) < 8, -1, POOL - 1) == own_row)
    edge_counts = dot(edge_member, ones)
    edge_slots = dot(edge_member, bkt_t[...]).astype(bf16)
    edge_sums = dot(edge_member, pt_ref[...])
    own_cols = jnp.transpose(jnp.broadcast_to(own_row.astype(f32), (128, ROWS)))
    inner_t = jnp.concatenate(
        [onehot(jnp.where(own_cols == POOL - 1.0, -1.0, own_cols) == lanes + k * 128.0) for k in range(POOL // 128)],
        axis=1,
    )
    last_cols = jnp.where(own_cols == POOL - 1.0, 1.0, 0.0)
    spilled_cols = jnp.where(own_cols < 0.0, 1.0, 0.0)
    for k in range(2):
        e_out[k, :, C:] = edge_counts[8 * k : 8 * k + 8]

    came = in2.at[pl.ds(0, FIRST)]
    pltpu.make_async_copy(came, came, recv2.at[0]).wait()
    slots = []
    for half in range(2):
        slots.append(returned(half))
        sums = dot(edge_slots, slots[half])
        high = sums.astype(bf16)
        both_parts = jnp.concatenate([high, (sums - high.astype(f32)).astype(bf16)], axis=0)
        parts = dot(both_parts, wout_ref[half * 128 : (half + 1) * 128])
        edge_sums = edge_sums + parts[:16] + parts[16:]
    for k in range(2):
        e_out[k, :, :C] = edge_sums[8 * k : 8 * k + 8]

    def edge(k, line):
        return pltpu.make_async_remote_copy(
            src_ref=e_out.at[k], dst_ref=e_in.at[k], send_sem=esend.at[k], recv_sem=erecv.at[k],
            device_id=(line // 4, line % 4), device_id_type=MESH,
        )

    to_previous = edge(0, (me + DEVS - 1) % DEVS)
    to_next = edge(1, (me + 1) % DEVS)

    @pl.when(me > 0)
    def _():
        to_previous.start()

    @pl.when(me == 0)
    def _():
        e_in[1] = jnp.zeros((8, C + 128), f32)

    @pl.when(me < DEVS - 1)
    def _():
        to_next.start()

    @pl.when(me == DEVS - 1)
    def _():
        e_in[0] = jnp.zeros((8, C + 128), f32)

    mixed = pt_ref[...].astype(f32)
    for half in range(2):
        attended = dot(bkt_t[...], slots[half]).astype(bf16)
        mixed = mixed + dot(attended, wout_ref[half * 128 : (half + 1) * 128])
    encoded = mixed.astype(bf16)

    def pool(sums, tallies):
        mean = sums / jnp.concatenate([tallies, tallies], axis=1)
        return gelu(layer_norm(dot(mean.astype(bf16), wpool_ref[...]))).astype(bf16)

    def lift(rows):
        return gelu(layer_norm(dot(rows, wup_ref[...]))).astype(bf16)

    pooled = pool(dot(member, encoded), counts)
    pooled_ref[...] = pooled
    skipped = gelu(layer_norm(dot(encoded, wskip_ref[...])))
    partial = skipped + dot(inner_t, lift(pooled))

    @pl.when(me > 0)
    def _():
        to_previous.wait_send()
        to_next.wait_recv()

    @pl.when(me < DEVS - 1)
    def _():
        to_next.wait_send()
        to_previous.wait_recv()

    shared = jnp.concatenate([e_out[1] + e_in[0], e_in[1] + e_out[0]], axis=0)
    shared_pooled = pool(shared[:, :C], jnp.maximum(shared[:, C:], 1.0))
    pooled_ref[POOL - 16 :] = jnp.where(iota((16, C2), 0) == 15, shared_pooled[:1], pooled[POOL - 16 :])
    shared_lifted = lift(shared_pooled).astype(f32)
    both = lambda v: jnp.concatenate([v, v], axis=1)
    picked = both(last_cols) * shared_lifted[:1] + both(spilled_cols) * shared_lifted[8:9]
    dec_ref[...] = (partial + picked).astype(bf16)

    most = out1.at[pl.ds(0, (DEVS - 1) * BLK)]
    pltpu.make_async_copy(most, most, send1).wait()
    most = out2.at[:FIRST]
    pltpu.make_async_copy(most, most, send2.at[0]).wait()
    for half in range(2):
        most = out2.at[FIRST : DEVS - 1, half]
        pltpu.make_async_copy(most, most, send2.at[1 + half]).wait()


def hand_out(pooled_ref, dec_ref, pooled_out, dec_out, sems):
    first = pltpu.make_async_copy(dec_ref, dec_out, sems.at[0])
    second = pltpu.make_async_copy(pooled_ref, pooled_out, sems.at[1])
    first.start()
    second.start()
    first.wait()
    second.wait()


def on_device(points, to_hilbert, parent, w_qkv, w_out, w_pool, w_up, w_skip):
    given = (points, to_hilbert.reshape(1, ROWS), parent.reshape(1, ROWS), w_qkv, w_out, w_pool, w_up, w_skip)
    vmem = pl.BlockSpec(memory_space=pltpu.VMEM)
    dma = pltpu.SemaphoreType.DMA
    held = [pltpu.with_memory_space_constraint(v, pltpu.HBM) for v in given]
    results = pl.pallas_call(
        kernel,
        out_shape=(pltpu.VMEM((POOL, C2), bf16), pltpu.VMEM((ROWS, C), bf16)),
        in_specs=[pl.BlockSpec(memory_space=pltpu.HBM)] * 8,
        out_specs=(vmem, vmem),
        scratch_shapes=[
            pltpu.VMEM((ROWS, C), bf16),
            pltpu.VMEM((1, ROWS), i32),
            pltpu.VMEM((1, ROWS), i32),
            pltpu.VMEM((C, 3 * C), bf16),
            pltpu.VMEM((C, C), bf16),
            pltpu.VMEM((C, C2), bf16),
            pltpu.VMEM((C2, C), bf16),
            pltpu.VMEM((C, C), bf16),
            pltpu.VMEM((DEVS * BLK, 128), bf16),
            pltpu.VMEM((DEVS * BLK, 128), bf16),
            pltpu.VMEM((DEVS, 2, CAP, 128), bf16),
            pltpu.VMEM((DEVS, 2, CAP, 128), bf16),
            pltpu.VMEM((ROWS, SLOTS), bf16),
            pltpu.VMEM((SLOTS, ROWS), bf16),
            pltpu.VMEM((C, C), bf16),
            pltpu.VMEM((C, C), bf16),
            pltpu.VMEM((2, ROWS, C), bf16),
            pltpu.VMEM((HEADS * 128, ROWS), bf16),
            pltpu.VMEM((C, 2 * ROWS), bf16),
            pltpu.VMEM((2 * ROWS, C), bf16),
            pltpu.VMEM((2 * ROWS, QUERIES), f32),
            pltpu.VMEM((2 * ROWS, QUERIES), f32),
            pltpu.VMEM((2 * ROWS, QUERIES), f32),
            pltpu.VMEM((2 * ROWS, QUERIES), f32),
            pltpu.VMEM((C, ROWS), bf16),
            pltpu.VMEM((HEADS // 2, WIDTH, QUERIES), f32),
            pltpu.VMEM((HEADS // 2, 8, QUERIES), f32),
            pltpu.VMEM((HEADS // 2, 8, QUERIES), f32),
            pltpu.VMEM((2, 8, C + 128), f32),
            pltpu.VMEM((2, 8, C + 128), f32),
            dma, dma, dma, dma((3,)), dma((3,)), dma((2,)), dma, dma, dma((2,)), dma((2,)), dma((8,)),
        ],
        compiler_params=pltpu.CompilerParams(
            collective_id=0, has_side_effects=True, vmem_limit_bytes=48 * 1024 * 1024
        ),
    )(*held)
    results = [pltpu.with_memory_space_constraint(v, pltpu.VMEM) for v in results]
    anywhere = pl.BlockSpec(memory_space=pl.ANY)
    return pl.pallas_call(
        hand_out,
        out_shape=(jax.ShapeDtypeStruct((POOL, C2), bf16), jax.ShapeDtypeStruct((ROWS, C), bf16)),
        in_specs=[vmem, vmem],
        out_specs=(anywhere, anywhere),
        scratch_shapes=[dma((2,))],
    )(*results)


def solution(mesh):
    rows = P(("pts", "mdl"), None)
    flat = P(("pts", "mdl"))
    return jax.shard_map(
        on_device,
        mesh=mesh,
        in_specs=(rows, flat, flat, P(), P(), P(), P(), P()),
        out_specs=(rows, rows),
        check_vma=False,
    )
```
